768 devices in a mesh: vert: 24 (over z, core), feat: 32 (over y, x).
Axes of the slice: x: 4, y: 8, z: 12, core: 2. Of those that a mesh axis runs over, the one named last changes fastest.
Arguments:
- node_feats: bfloat16 [128, 196608], P('feat', 'vert'), may hold values from -6 to 6
- w_self: bfloat16 [128, 256], replicated, may hold values from -0.5 to 0.5
- w_neigh: bfloat16 [128, 256], replicated, may hold values from -6 to 6
- out_bias: float32 [256], replicated, may hold values from -3 to 3
- adjacency: bfloat16 [73728, 128, 128], P(('vert', 'feat')), may hold values from 0.0099487305 to 1
- block_dst: int32 [73728], P(('vert', 'feat')), may hold values from 0 to 1, as said below
- block_src: int32 [73728], P(('vert', 'feat')), may hold values from 0 to 111, as said below
- block_count: int32 [768], P(('vert', 'feat')), may hold values from 49 to 96, as said below
- send_list: int32 [24, 24, 2], P('vert'), may hold values from 0 to 63, as said below
- grad_out: bfloat16 [196608, 256], P(('vert', 'feat')), may hold values from -6 to 6
Outputs:
- activated: bfloat16 [196608, 256], P(('vert', 'feat'))
- grad_feats: float32 [128, 196608], P('feat', 'vert')
- grad_self: float32 [128, 256], replicated
- grad_neigh: float32 [128, 256], replicated
- grad_bias: float32 [256], replicated
The draws below stay inside these ranges and needn't reach their ends.
Inputs may be any that keep to these rules, and one draw needn't show every extreme that they name: `block_count`: some device has exactly 96 live blocks; blocks past a device's count are padding. `block_dst`: the first 2 blocks of every device have destination t, t = 0 to 1. `block_src`: the first 2 blocks of member m have source m * 2 + t. Below 64: a tile of the own slab; else 64 + p * 2 + s, slot s of what slab p sends, with p never the own slab. `send_list`: entry [p, r, s] is a tile of slab p, counted within slab p.
All inputs are finite; a program needn't handle non-finite values.
Results may differ from the reference program's by a relative error of at most 0.015.
Values may be sent and summed in bfloat16 or wider, within the bound.
No kernel may reach another device: no remote copies, remote signals or barrier semaphores. Data moves between devices by JAX's collectives and lax.ppermute only.
A program may use at most 32 MiB of HBM per device.

```python
import math
import jax
import jax.numpy as jnp
from jax import lax

F = 128
H = 256
TILE = 128
SLOTS = 2
DT = 2
BPD = 96
TB = 64
V = 196608
NBLK = 73728
N_VERT = 24
N_FEAT = 32


def layout_tables(key):
    subkeys = jax.random.split(key, 7)
    devices = N_VERT * N_FEAT
    lowest = DT + (BPD - DT) // 2
    counts = jax.random.randint(subkeys[0], (devices,), lowest, BPD + 1)
    fullest = jax.random.randint(subkeys[1], (), 0, devices)
    positions = jnp.arange(devices)
    counts = jnp.where(positions == (fullest + 1) % devices, lowest, counts)
    counts = jnp.where(positions == fullest, BPD, counts).astype(jnp.int32)
    extra_blocks = BPD - DT
    member = positions % N_FEAT
    slab_of = positions // N_FEAT
    diag_dst = jnp.broadcast_to(jnp.arange(DT, dtype=jnp.int32)[None, :], (devices, DT))
    diag_src = (member[:, None] * DT + jnp.arange(DT)[None, :]).astype(jnp.int32)
    dst_extra = jax.random.randint(subkeys[2], (devices, extra_blocks), 0, DT)
    remote = jax.random.randint(subkeys[3], (devices, extra_blocks), 0, 2)
    local_src = jax.random.randint(subkeys[4], (devices, extra_blocks), 0, TB)
    peer_shift = jax.random.randint(subkeys[5], (devices, extra_blocks), 1, N_VERT)
    slot_pick = jax.random.randint(subkeys[6], (devices, extra_blocks), 0, SLOTS)
    peer_slab = (slab_of[:, None] + peer_shift) % N_VERT
    src_extra = jnp.where(remote == 1, TB + peer_slab * SLOTS + slot_pick, local_src)
    forced = (slab_of[:, None] == 0) & (member[:, None] == 0) & (jnp.arange(extra_blocks)[None, :] == 0)
    src_extra = jnp.where(forced, TB + (N_VERT - 1) * SLOTS + SLOTS - 1, src_extra)
    dst_all = jnp.concatenate([diag_dst, dst_extra], axis=1).reshape(-1).astype(jnp.int32)
    src_all = jnp.concatenate([diag_src, src_extra], axis=1).reshape(-1).astype(jnp.int32)
    return (counts, dst_all, src_all)


def draw_block_dst(key, part):
    counts, dst_all, src_all = layout_tables(key)
    return dst_all


def draw_block_src(key, part):
    counts, dst_all, src_all = layout_tables(key)
    return src_all


def draw_block_count(key, part):
    counts, dst_all, src_all = layout_tables(key)
    return counts


def draw_send_list(key, part):
    key = jax.random.fold_in(key, 11)
    picked = jax.random.randint(key, (N_VERT, N_VERT, SLOTS), 0, TB)
    picked = picked.at[0, 1, 0].set(TB - 1)
    picked = picked.at[0, 1, SLOTS - 1].set(0)
    return picked.astype(jnp.int32)


def steps_of(rng, extent, cuts, smallest, largest):
    level = 1.0
    for axis_at, parts in cuts:
        heights = jax.random.uniform(jax.random.fold_in(jax.random.fold_in(rng, 6), axis_at), (parts,), jnp.float32, smallest / len(cuts), largest / len(cuts))
        level = level * jnp.repeat(jnp.exp(heights), extent[axis_at] // parts).reshape((-1,) + (1,) * (len(extent) - 1 - axis_at))
    return level


def bell_draw(own_key, extent, width, reach, shards=(), kind=jnp.bfloat16):
    array = jax.random.normal(own_key, extent, jnp.float32) * width
    if len(shards) > 0:
        array = steps_of(own_key, extent, shards, -0.22, 0.18) * array
    return jnp.clip(array, min=-reach, max=reach).astype(kind)


def setup_inputs(seed: int = 0) -> dict:
    key_list = jax.random.split(jax.random.key(seed), 11)
    return {
        "node_feats": bell_draw(key_list[0], (F, V), 1.0, 6.0, ((0, 32), (1, 24))),
        "w_self": bell_draw(key_list[1], (F, H), F ** -0.5, 0.5),
        "w_neigh": bell_draw(key_list[2], (F, H), (max(F // 128, 1)) ** -0.5, 6.0),
        "out_bias": bell_draw(key_list[3], (H,), 0.5, 3.0, (), jnp.float32),
        "adjacency": jnp.clip(jnp.exp(math.log(1.0) - 4.61031033 * jax.random.uniform(key_list[4], (NBLK, TILE, TILE), jnp.float32) ** steps_of(key_list[4], (NBLK, TILE, TILE), ((0, 768),), -0.2, 0.2)), 0.0099487305, 1.0).astype(jnp.bfloat16),
        "block_dst": draw_block_dst(jax.random.fold_in(key_list[10], 71), 0),
        "block_src": draw_block_src(jax.random.fold_in(key_list[10], 71), 0),
        "block_count": draw_block_count(jax.random.fold_in(key_list[10], 71), 0),
        "send_list": draw_send_list(jax.random.fold_in(key_list[10], 71), 0),
        "grad_out": bell_draw(key_list[9], (V, H), 1.0, 6.0, ((0, 768),)),
    }


def block_weights(adjacency, block_dst, live_count, tile_count):
    blocks = adjacency.shape[0]
    living = (jnp.arange(blocks) < live_count).astype(jnp.float32)
    placing = (block_dst[:, None] == jnp.arange(tile_count)[None, :]).astype(jnp.float32) * living[:, None]
    row_sums = jnp.sum(adjacency.astype(jnp.float32), axis=2)
    degree = jnp.einsum('bt,bi->ti', placing, row_sums, precision=lax.Precision.HIGHEST)
    return living, placing, degree


def gather_sum(src_table, adjacency, block_src, placing):
    sources = jnp.take(src_table, block_src, axis=1)
    contrib = jnp.einsum('bik,cbk->cbi', adjacency.astype(jnp.float32), sources.astype(jnp.float32))
    return jnp.einsum('bt,cbi->cti', placing, contrib, precision=lax.Precision.HIGHEST)


def reference(node_feats, w_self, w_neigh, out_bias, adjacency, block_dst, block_src, block_count, send_list, grad_out):
    feat_tiles = node_feats.reshape(F, N_VERT, TB, TILE)
    peer_rows = jnp.arange(N_VERT)[:, None]
    table_tiles = TB + N_VERT * SLOTS
    adj_split = adjacency.reshape(N_VERT, N_FEAT, BPD, TILE, TILE)
    dst_split = block_dst.reshape(N_VERT, N_FEAT, BPD)
    src_split = block_src.reshape(N_VERT, N_FEAT, BPD)
    count_split = block_count.reshape(N_VERT, N_FEAT)
    mean_slabs = []
    degrees = []
    for slab_index in range(N_VERT):
        incoming = feat_tiles[:, peer_rows, send_list[:, slab_index, :]]
        src_table = jnp.concatenate([feat_tiles[:, slab_index], incoming.reshape(F, N_VERT * SLOTS, TILE)], axis=1)

        def member_mean(inputs):
            block_adj, dst_here, src_here, live_count = inputs
            living, placing, degree = block_weights(block_adj, dst_here, live_count, DT)
            summed = gather_sum(src_table, block_adj, src_here, placing)
            return (summed / degree[None]).astype(jnp.bfloat16), degree

        mean_parts, degree_parts = lax.map(member_mean, (adj_split[slab_index], dst_split[slab_index],
                                                         src_split[slab_index], count_split[slab_index]))
        mean_slabs.append(jnp.transpose(mean_parts, (1, 0, 2, 3)).reshape(F, TB * TILE))
        degrees.append(degree_parts)
    neigh_mean = jnp.concatenate(mean_slabs, axis=1)
    preact = (jnp.dot(node_feats.T, w_self, preferred_element_type=jnp.float32)
              + jnp.dot(neigh_mean.T, w_neigh, preferred_element_type=jnp.float32) + out_bias)
    activated = jax.nn.silu(preact).astype(jnp.bfloat16)
    sigmoid_pre = jax.nn.sigmoid(preact)
    grad_pre = (grad_out.astype(jnp.float32) * sigmoid_pre * (1.0 + preact * (1.0 - sigmoid_pre))).astype(jnp.bfloat16)
    grad_self = jnp.dot(node_feats, grad_pre, preferred_element_type=jnp.float32)
    grad_neigh = jnp.dot(neigh_mean, grad_pre, preferred_element_type=jnp.float32)
    grad_bias = jnp.sum(grad_pre.astype(jnp.float32), axis=0)
    contract_last = (((1,), (1,)), ((), ()))
    from_self = lax.dot_general(w_self, grad_pre, contract_last, preferred_element_type=jnp.float32)
    from_mean = lax.dot_general(w_neigh, grad_pre, contract_last, preferred_element_type=jnp.float32)
    self_split = from_self.reshape(F, N_VERT, N_FEAT, DT, TILE)
    mean_split = from_mean.reshape(F, N_VERT, N_FEAT, DT, TILE)
    grad_tiles = jnp.zeros((F, N_VERT, TB, TILE), jnp.float32)
    for slab_index in range(N_VERT):
        def member_terms(running, inputs):
            block_adj, dst_here, src_here, live_count, degree, own_self, own_mean, member = inputs
            living = (jnp.arange(BPD) < live_count).astype(jnp.float32)
            grad_mean = (own_mean / degree[None]).astype(jnp.bfloat16)
            at_dst = jnp.take(grad_mean, dst_here, axis=1)
            backward = jnp.einsum('bik,cbi->cbk', block_adj.astype(jnp.float32), at_dst.astype(jnp.float32))
            backward = backward * living[None, :, None]
            src_onehot = (src_here[:, None] == jnp.arange(table_tiles)[None, :]).astype(jnp.float32)
            dev_terms = jnp.einsum('bn,cbk->cnk', src_onehot, backward, precision=lax.Precision.HIGHEST)
            first_tile = (member * DT).astype(jnp.int32)
            placed = lax.dynamic_slice_in_dim(dev_terms, first_tile, DT, 1) + own_self
            dev_terms = lax.dynamic_update_slice_in_dim(dev_terms, placed, first_tile, 1)
            rounded = lax.optimization_barrier(dev_terms.astype(jnp.bfloat16)).astype(jnp.float32)
            return running + rounded, None

        inputs = (adj_split[slab_index], dst_split[slab_index], src_split[slab_index], count_split[slab_index],
                  degrees[slab_index], jnp.moveaxis(self_split[:, slab_index], 1, 0),
                  jnp.moveaxis(mean_split[:, slab_index], 1, 0), jnp.arange(N_FEAT, dtype=jnp.int32))
        slab_terms, _ = lax.scan(member_terms, jnp.zeros((F, table_tiles, TILE), jnp.float32), inputs)
        grad_tiles = grad_tiles.at[:, slab_index].add(slab_terms[:, :TB])
        away = slab_terms[:, TB:].reshape(F, N_VERT, SLOTS, TILE)
        grad_tiles = grad_tiles.at[:, peer_rows, send_list[:, slab_index, :]].add(away)
    grad_feats = grad_tiles.reshape(F, V)
    return activated, grad_feats, grad_self, grad_neigh, grad_bias
```

```python
import functools

import jax
import jax.numpy as jnp
from jax import lax
from jax.experimental import pallas as pl
from jax.experimental.pallas import tpu as pltpu
from jax.sharding import Mesh
from jax.sharding import PartitionSpec as P

X, Y, Z, C = 4, 8, 12, 2
MEMBERS = X * Y
SLABS = Z * C
F = 128
H = 256
TILE = 128
SLOTS = 2
OWN = 64
AWAY = SLABS * SLOTS
TABLE = OWN + AWAY
ROWS = F // MEMBERS
BPD = 96
OWNED = 2 * TILE
GRADS = 5
WIDE = GRADS * TILE
COLS = TABLE * TILE
FULL = COLS + 2 * WIDE
GROUP = 8

BF = jnp.bfloat16
F32 = jnp.float32
VMEM = pl.BlockSpec(memory_space=pltpu.VMEM)
SMEM = pl.BlockSpec(memory_space=pltpu.SMEM)
LIMIT = 40 * 1024 * 1024


def call(body, ins, outs, scratch=()):
    return pl.pallas_call(
        body,
        in_specs=ins,
        out_specs=jax.tree.map(lambda _: VMEM, outs),
        out_shape=outs,
        scratch_shapes=scratch,
        compiler_params=pltpu.CompilerParams(vmem_limit_bytes=LIMIT),
    )


def struct(shape, dtype):
    return jax.ShapeDtypeStruct(shape, dtype)


def lanes(at):
    return pl.ds(pl.multiple_of(at * TILE, TILE), TILE)


def pick_kernel(send, feats, out):
    for slab in range(SLABS):
        for slot in range(SLOTS):
            tile = feats[:, lanes(send[slab * SLOTS + slot])]
            out[slab, slot * ROWS : (slot + 1) * ROWS, :] = tile


def table_kernel(feats, incoming, out):
    out[:, : OWN * TILE] = feats[...]
    for slab in range(SLABS):
        for slot in range(SLOTS):
            at = (OWN + slab * SLOTS + slot) * TILE
            out[:, at : at + TILE] = incoming[slab, slot * ROWS : (slot + 1) * ROWS, :]


def dot(a, b, ca, cb):
    return lax.dot_general(a, b, (((ca,), (cb,)), ((), ())), preferred_element_type=F32)


def split(value):
    high = value.astype(BF)
    return high, (value - high.astype(F32)).astype(BF)


def iota(shape, axis):
    return lax.broadcasted_iota(jnp.int32, shape, axis)


def layer_kernel(
    src, dst, count, first, table, adj, w_self, w_neigh, bias, grad_out, act, out, gathered, terms
):
    live = count[0]
    groups = lax.div(live + (GROUP - 1), GROUP)
    gathered[...] = jnp.zeros_like(gathered)
    ones = jnp.ones((8, GROUP * TILE), BF)

    def forward(g, carry):
        left, right = [], []
        for j in range(GROUP):
            b = g * GROUP + j
            left.append(table[:, lanes(src[b])])
            block = adj[b]
            alive = b < live
            halves = []
            for t in range(2):
                keep = jnp.where(jnp.logical_and(alive, dst[b] == t), 1.0, 0.0)
                halves.append(block * jnp.full((TILE, TILE), keep, F32).astype(BF))
            right.append(jnp.concatenate(halves, axis=0))
        lhs = jnp.concatenate([jnp.concatenate(left, axis=1), ones], axis=0)
        gathered[...] += dot(lhs, jnp.concatenate(right, axis=1), 1, 1)
        return carry

    lax.fori_loop(0, groups, forward, 0)
    degree = gathered[F : F + 1, :]
    mean = (gathered[:F, :] / degree).astype(BF)
    start = pl.multiple_of(first[0], OWNED)
    own = table[:, pl.ds(start, OWNED)]
    pre = dot(own, w_self[...], 0, 0) + dot(mean, w_neigh[...], 0, 0) + bias[...]
    sig = jax.nn.sigmoid(pre)
    act[...] = (pre * sig).astype(BF)
    grad_pre = (grad_out[...].astype(F32) * sig * (1.0 + pre * (1.0 - sig))).astype(BF)
    part_bias = jnp.sum(grad_pre.astype(F32), axis=0, keepdims=True)

    row, col = iota((F, F), 0), iota((F, F), 1)
    x_of, y_of = (col // ROWS) % X, col // (ROWS * X)
    order = (row == x_of * (Y * ROWS) + y_of * ROWS + col % ROWS).astype(F32).astype(BF)

    def reorder(value):
        return dot(order, value, 1, 0).astype(BF)

    for k, value in enumerate((own, mean)):
        high, low = split(dot(value, grad_pre, 1, 0))
        at = COLS + k * H
        out[:, at : at + H] = reorder(high)
        out[:, at + WIDE : at + WIDE + H] = reorder(low)
    per = H // MEMBERS
    mine = iota((F, H), 1) // per == iota((F, H), 0) // ROWS
    squeeze = (iota((H, TILE), 0) % per == iota((H, TILE), 1)).astype(F32).astype(BF)
    for k, value in enumerate(split(part_bias)):
        spread = jnp.where(mine, value.astype(F32), 0.0).astype(BF)
        at = COLS + k * WIDE + 2 * H
        out[:, at : at + TILE] = reorder(dot(spread, squeeze, 1, 0).astype(BF))

    from_self = dot(reorder(w_self[...]), grad_pre, 1, 1)
    grad_mean = (dot(reorder(w_neigh[...]), grad_pre, 1, 1) / degree).astype(BF)
    pair = (grad_mean[:, :TILE], grad_mean[:, TILE:])
    terms[...] = jnp.zeros_like(terms)
    terms[:, pl.ds(start, OWNED)] = from_self

    def backward(g, carry):
        for j in range(GROUP):
            b = g * GROUP + j
            keep = jnp.where(b < live, 1.0, 0.0)
            second = jnp.full((F, TILE), dst[b], jnp.int32) == 1
            value = jnp.where(second, pair[1].astype(F32), pair[0].astype(F32)) * keep
            terms[:, lanes(src[b])] += dot(value.astype(BF), adj[b], 1, 0)
        return carry

    lax.fori_loop(0, groups, backward, 0)

    def narrow(n, carry):
        at = pl.ds(pl.multiple_of(n * 1024, 1024), 1024)
        out[:, at] = terms[:, at].astype(BF)
        return carry

    lax.fori_loop(0, COLS // 1024, narrow, 0)


def first_sum_kernel(parts, out):
    rows = F // X

    def total(at):
        return sum(parts[x * rows : (x + 1) * rows, at].astype(F32) for x in range(X))

    def put(value, at):
        for y in range(Y):
            out[y, :, at] = value[y * ROWS : (y + 1) * ROWS, :]

    def step(n, carry):
        at = pl.ds(pl.multiple_of(n * 512, 512), 512)
        put(total(at).astype(BF), at)
        return carry

    lax.fori_loop(0, COLS // 512, step, 0)
    high_at, low_at = pl.ds(COLS, WIDE), pl.ds(COLS + WIDE, WIDE)
    high, low = split(total(high_at) + total(low_at))
    put(high, high_at)
    put(low, low_at)


def second_sum_kernel(parts, own, away):
    def total(at, width):
        return sum(parts[y, :, at : at + width].astype(F32) for y in range(Y))

    for at in range(0, OWN * TILE, 1024):
        own[:, at : at + 1024] = total(at, 1024)
    for slab in range(SLABS):
        for slot in range(SLOTS):
            tile = total((OWN + slab * SLOTS + slot) * TILE, TILE)
            away[slab, slot * ROWS : (slot + 1) * ROWS, :] = tile.astype(BF)
    both = split(total(COLS, WIDE) + total(COLS + WIDE, WIDE))
    base = SLOTS * ROWS
    for value in both:
        for k in range(GRADS):
            piece = value[:, k * TILE : (k + 1) * TILE]
            for slab in range(SLABS):
                away[slab, base : base + ROWS, :] = piece
            base += ROWS


def land_kernel(send, own, back, out, grads):
    out[...] = own[...]
    for slab in range(SLABS):
        for slot in range(SLOTS):
            tile = back[slab, slot * ROWS : (slot + 1) * ROWS, :].astype(F32)
            out[:, lanes(send[slab * SLOTS + slot])] += tile
    base = SLOTS * ROWS
    for k in range(GRADS):
        at = base + k * ROWS
        low = at + GRADS * ROWS
        value = sum(
            back[slab, at : at + ROWS, :].astype(F32) + back[slab, low : low + ROWS, :].astype(F32)
            for slab in range(SLABS)
        )
        for m in range(MEMBERS):
            grads[m, :, k * TILE : (k + 1) * TILE] = value


def local(
    node_feats,
    w_self,
    w_neigh,
    out_bias,
    adjacency,
    block_dst,
    block_src,
    block_count,
    send_list,
    grad_out,
):
    send = send_list.reshape(-1)
    first = (lax.axis_index(("y", "x")) * OWNED).astype(jnp.int32).reshape(1)
    outgoing = call(pick_kernel, [SMEM, VMEM], struct((SLABS, SLOTS * ROWS, TILE), BF))(
        send, node_feats
    )
    incoming = lax.all_to_all(outgoing, ("z", "c"), 0, 0, tiled=True)
    table = call(table_kernel, [VMEM, VMEM], struct((ROWS, COLS), BF))(node_feats, incoming)
    table = lax.all_gather(table, "x", axis=0, tiled=True)
    table = lax.all_gather(table, "y", axis=0, tiled=True)
    activated, terms = call(
        layer_kernel,
        [SMEM] * 4 + [VMEM] * 6,
        (struct((OWNED, H), BF), struct((F, FULL), BF)),
        (pltpu.VMEM((F + 8, OWNED), F32), pltpu.VMEM((F, COLS), F32)),
    )(
        block_src,
        block_dst,
        block_count,
        first,
        table,
        adjacency,
        w_self,
        w_neigh,
        out_bias.reshape(1, H),
        grad_out,
    )
    terms = lax.all_to_all(terms, "x", 0, 0, tiled=True)
    terms = call(first_sum_kernel, [VMEM], struct((Y, ROWS, FULL), BF))(terms)
    terms = lax.all_to_all(terms, "y", 0, 0, tiled=True)
    own, away = call(
        second_sum_kernel,
        [VMEM],
        (
            struct((ROWS, OWN * TILE), F32),
            struct((SLABS, SLOTS * ROWS + 2 * GRADS * ROWS, TILE), BF),
        ),
    )(terms)
    back = lax.all_to_all(away, ("z", "c"), 0, 0, tiled=True)
    grad_feats, grads = call(
        land_kernel,
        [SMEM, VMEM, VMEM],
        (struct((ROWS, OWN * TILE), F32), struct((MEMBERS, ROWS, WIDE), F32)),
    )(send, own, back)
    grads = lax.all_to_all(grads, ("y", "x"), 0, 0, tiled=True)
    grad_self = grads[:, :, :H].reshape(F, H)
    grad_neigh = grads[:, :, H : 2 * H].reshape(F, H)
    grad_bias = grads[:, 0, 2 * H : 2 * H + H // MEMBERS].reshape(H)
    return activated, grad_feats, grad_self, grad_neigh, grad_bias


def solution(mesh):
    grid = Mesh(mesh.devices.reshape(Z, C, Y, X), ("z", "c", "y", "x"))
    vert, feat = ("z", "c"), ("y", "x")
    every = vert + feat
    in_specs = (
        P(feat, vert),
        P(),
        P(),
        P(),
        P(every, None, None),
        P(every),
        P(every),
        P(every),
        P(vert, None, None),
        P(every, None),
    )
    out_specs = (P(every, None), P(feat, vert), P(), P(), P())
    return jax.shard_map(local, mesh=grid, in_specs=in_specs, out_specs=out_specs, check_vma=False)
```

```python
import functools

import jax
import jax.numpy as jnp
from jax import lax
from jax.experimental import pallas as pl
from jax.experimental.pallas import tpu as pltpu
from jax.sharding import Mesh
from jax.sharding import PartitionSpec as P

X, Y, Z, C = 4, 8, 12, 2
MEMBERS = X * Y
SLABS = Z * C
F = 128
H = 256
TILE = 128
SLOTS = 2
OWN = 64
AWAY = SLABS * SLOTS
TABLE = OWN + AWAY
ROWS = F // MEMBERS
BPD = 96
OWNED = 2 * TILE
COLS = TABLE * TILE
OWN_COLS = OWN * TILE
AWAY_COLS = AWAY * TILE
CHUNK = 24
GRAD_ROWS = SLABS * CHUNK
GROUP = 8
FETCHES = 4
FETCH = BPD // FETCHES

BF = jnp.bfloat16
F32 = jnp.float32
VMEM = pl.BlockSpec(memory_space=pltpu.VMEM)
SMEM = pl.BlockSpec(memory_space=pltpu.SMEM)
HBM = pl.BlockSpec(memory_space=pltpu.HBM)
LIMIT = 40 * 1024 * 1024
FULL_LIMIT = 62 * 1024 * 1024


def call(body, ins, outs, scratch=(), places=None, limit=LIMIT):
    return pl.pallas_call(
        body,
        in_specs=ins,
        out_specs=jax.tree.map(lambda _: VMEM, outs) if places is None else places,
        out_shape=outs,
        scratch_shapes=scratch,
        compiler_params=pltpu.CompilerParams(vmem_limit_bytes=limit),
    )


def struct(shape, dtype):
    return jax.ShapeDtypeStruct(shape, dtype)


def lanes(at):
    return pl.ds(pl.multiple_of(at * TILE, TILE), TILE)


def pick_kernel(send, feats, out):
    for slab in range(SLABS):
        for slot in range(SLOTS):
            tile = feats[:, lanes(send[slot, slab])]
            out[slab, slot * ROWS : (slot + 1) * ROWS, :] = tile


def table_kernel(feats, incoming, out):
    out[:, :OWN_COLS] = feats[...]
    for slab in range(SLABS):
        for slot in range(SLOTS):
            at = OWN_COLS + (slab * SLOTS + slot) * TILE
            out[:, at : at + TILE] = incoming[slab, slot * ROWS : (slot + 1) * ROWS, :]


def dot(a, b, ca, cb):
    return lax.dot_general(a, b, (((ca,), (cb,)), ((), ())), preferred_element_type=F32)


def iota(shape, axis):
    return lax.broadcasted_iota(jnp.int32, shape, axis)


def layer_kernel(
    src,
    dst,
    count,
    first,
    table_hbm,
    adj_hbm,
    w_self_hbm,
    w_neigh_hbm,
    bias_hbm,
    grad_out_hbm,
    act,
    out_hbm,
    grads,
    out,
    table,
    adj,
    w_self,
    w_neigh,
    bias,
    grad_out,
    gathered,
    terms,
    sems,
):
    def fetch(k, source, target):
        copy = pltpu.make_async_copy(source, target, sems.at[k])
        copy.start()
        return copy

    get_table = fetch(0, table_hbm, table)
    get_adj = [
        fetch(1 + k, adj_hbm.at[pl.ds(k * FETCH, FETCH)], adj.at[pl.ds(k * FETCH, FETCH)])
        for k in range(FETCHES)
    ]
    rest = [
        fetch(1 + FETCHES + k, source, target)
        for k, (source, target) in enumerate(
            (
                (w_self_hbm, w_self),
                (w_neigh_hbm, w_neigh),
                (bias_hbm, bias),
                (grad_out_hbm, grad_out),
            )
        )
    ]

    row, col = iota((F, F), 0), iota((F, F), 1)

    x_of, y_of = (col // ROWS) % X, col // (ROWS * X)
    order = (row == x_of * (Y * ROWS) + y_of * ROWS + col % ROWS).astype(F32).astype(BF)
    live = count[0]
    gathered[...] = jnp.zeros_like(gathered)
    ones = jnp.ones((8, GROUP * TILE), BF)
    get_table.wait()

    def forward(g, carry):
        left, right = [], []
        for j in range(GROUP):
            b = g * GROUP + j
            left.append(table[:, lanes(src[b])])
            block = adj[b]
            alive = b < live
            halves = []
            for t in range(2):
                keep = jnp.where(jnp.logical_and(alive, dst[b] == t), 1.0, 0.0)
                halves.append(block * jnp.full((TILE, TILE), keep, F32).astype(BF))
            right.append(jnp.concatenate(halves, axis=0))
        lhs = jnp.concatenate([jnp.concatenate(left, axis=1), ones], axis=0)
        gathered[...] += dot(lhs, jnp.concatenate(right, axis=1), 1, 1)
        return carry

    groups = lax.div(live + (GROUP - 1), GROUP)
    per = FETCH // GROUP
    for k in range(FETCHES):
        get_adj[k].wait()
        lax.fori_loop(k * per, jnp.minimum(groups, (k + 1) * per), forward, 0)
    for copy in rest:
        copy.wait()
    degree = gathered[F : F + 1, :]
    mean = (gathered[:F, :] / degree).astype(BF)
    start = pl.multiple_of(first[0], OWNED)
    own = table[:, pl.ds(start, OWNED)]
    pre = dot(own, w_self[...], 0, 0) + dot(mean, w_neigh[...], 0, 0) + bias[...]
    sig = jax.nn.sigmoid(pre)
    act[...] = (pre * sig).astype(BF)
    grad_pre = (grad_out[...].astype(F32) * sig * (1.0 + pre * (1.0 - sig))).astype(BF)

    at = 0
    for value in (own, mean):
        part = dot(value, grad_pre, 1, 0)
        for k in range(H // TILE):
            grads[at : at + F, :] = part[:, k * TILE : (k + 1) * TILE]
            at += F
    part_bias = jnp.sum(grad_pre.astype(F32), axis=0, keepdims=True)
    grads[at:, :] = jnp.zeros((GRAD_ROWS - at, TILE), F32)
    for k in range(H // TILE):
        grads[at + k : at + k + 1, :] = part_bias[:, k * TILE : (k + 1) * TILE]

    def reorder(value):
        return dot(order, value, 1, 0).astype(BF)

    from_self = dot(reorder(w_self[...]), grad_pre, 1, 1)
    grad_mean = (dot(reorder(w_neigh[...]), grad_pre, 1, 1) / degree).astype(BF)
    pair = (grad_mean[:, :TILE], grad_mean[:, TILE:])
    terms[...] = jnp.zeros_like(terms)
    terms[:, pl.ds(start, OWNED)] = from_self

    def backward(g, carry):
        for j in range(GROUP):
            b = g * GROUP + j
            keep = jnp.where(b < live, 1.0, 0.0)
            second = jnp.full((F, TILE), dst[b], jnp.int32) == 1
            value = jnp.where(second, pair[1].astype(F32), pair[0].astype(F32)) * keep
            terms[:, lanes(src[b])] += dot(value.astype(BF), adj[b], 1, 0)
        return carry

    lax.fori_loop(0, groups, backward, 0)

    def narrow(n, carry):
        at = pl.ds(pl.multiple_of(n * 1024, 1024), 1024)
        out[:, at] = terms[:, at].astype(BF)
        return carry

    lax.fori_loop(0, COLS // 1024, narrow, 0)
    put = pltpu.make_async_copy(out, out_hbm, sems.at[0])
    put.start()
    put.wait()


def cut_kernel(terms, out):
    for y in range(Y):
        out[y] = terms[y * ROWS : (y + 1) * ROWS, :]


def spread_kernel(parts, out):
    total = sum(parts[k] for k in range(SLABS))
    for m in range(MEMBERS):
        out[m] = total


def sum_kernel(parts, grads, own, away):
    def total(at, width):
        return sum(parts[y, :, at : at + width].astype(F32) for y in range(Y))

    for at in range(0, OWN_COLS, 1024):
        own[:, at : at + 1024] = total(at, 1024)
    whole = sum(grads[m] for m in range(MEMBERS)).astype(BF)
    for slab in range(SLABS):
        for slot in range(SLOTS):
            tile = total(OWN_COLS + (slab * SLOTS + slot) * TILE, TILE)
            away[slab, slot * ROWS : (slot + 1) * ROWS, :] = tile.astype(BF)
        away[slab, SLOTS * ROWS :, :] = whole


def land_kernel(send, own, back, out, grad_self, grad_neigh, grad_bias):
    out[...] = own[...]
    for slab in range(SLABS):
        for slot in range(SLOTS):
            tile = back[slab, slot * ROWS : (slot + 1) * ROWS, :].astype(F32)
            out[:, lanes(send[slot, slab])] += tile
    for slab in range(SLABS):
        value = back[slab, SLOTS * ROWS :, :].astype(F32)
        for k in range(0, CHUNK, 8):
            block, at = divmod(slab * CHUNK + k, F)
            if block < 4:
                target = (grad_self, grad_neigh)[block // 2]
                lane = (block % 2) * TILE
                target[at : at + 8, lane : lane + TILE] = value[k : k + 8]
            elif at == 0:
                for half in range(2):
                    grad_bias[:, half * TILE : (half + 1) * TILE] = value[k + half : k + half + 1]


def local(
    node_feats,
    w_self,
    w_neigh,
    out_bias,
    adjacency,
    block_dst,
    block_src,
    block_count,
    send_list,
    grad_out,
):
    vert, feat = ("z", "c"), ("y", "x")
    send = jnp.swapaxes(send_list[0], 0, 1)
    first = (lax.axis_index(feat) * OWNED).astype(jnp.int32).reshape(1)
    outgoing = call(pick_kernel, [SMEM, VMEM], struct((SLABS, SLOTS * ROWS, TILE), BF))(
        send, node_feats
    )
    incoming = lax.all_to_all(outgoing, vert, 0, 0, tiled=True)
    table = call(table_kernel, [VMEM, VMEM], struct((ROWS, COLS), BF))(node_feats, incoming)
    table = lax.all_gather(table, "x", axis=0, tiled=True)
    table = lax.all_gather(table, "y", axis=0, tiled=True)
    activated, terms, grads = call(
        layer_kernel,
        [SMEM] * 4 + [HBM] * 6,
        (struct((OWNED, H), BF), struct((F, COLS), BF), struct((GRAD_ROWS, TILE), F32)),
        (
            pltpu.VMEM((F, COLS), BF),
            pltpu.VMEM((F, COLS), BF),
            pltpu.VMEM((BPD, TILE, TILE), BF),
            pltpu.VMEM((F, H), BF),
            pltpu.VMEM((F, H), BF),
            pltpu.VMEM((1, H), F32),
            pltpu.VMEM((OWNED, H), BF),
            pltpu.VMEM((F + 8, OWNED), F32),
            pltpu.VMEM((F, COLS), F32),
            pltpu.SemaphoreType.DMA((1 + FETCHES + 4,)),
        ),
        (VMEM, HBM, VMEM),
        FULL_LIMIT,
    )(
        block_src,
        block_dst,
        block_count,
        first,
        table,
        adjacency,
        w_self,
        w_neigh,
        out_bias.reshape(1, H),
        grad_out,
    )
    terms = lax.psum_scatter(terms, "x", scatter_dimension=0, tiled=True)
    grads = grads.reshape(SLABS, CHUNK, TILE)
    grads = lax.all_to_all(grads, vert, 0, 0, tiled=True)
    grads = call(spread_kernel, [VMEM], struct((MEMBERS, CHUNK, TILE), F32))(grads)
    grads = lax.all_to_all(grads, feat, 0, 0, tiled=True)
    terms, grads = lax.optimization_barrier((terms, grads))
    terms = call(cut_kernel, [VMEM], struct((Y, ROWS, COLS), BF))(terms)
    terms = lax.all_to_all(terms, "y", 0, 0, tiled=True)
    own, away = call(
        sum_kernel,
        [VMEM, VMEM],
        (struct((ROWS, OWN_COLS), F32), struct((SLABS, SLOTS * ROWS + CHUNK, TILE), BF)),
    )(terms, grads)
    back = lax.all_to_all(away, vert, 0, 0, tiled=True)
    grad_feats, grad_self, grad_neigh, grad_bias = call(
        land_kernel,
        [SMEM, VMEM, VMEM],
        (
            struct((ROWS, OWN_COLS), F32),
            struct((F, H), F32),
            struct((F, H), F32),
            struct((1, H), F32),
        ),
    )(send, own, back)
    return activated, grad_feats, grad_self, grad_neigh, grad_bias.reshape(H)


def solution(mesh):
    grid = Mesh(mesh.devices.reshape(Z, C, Y, X), ("z", "c", "y", "x"))
    vert, feat = ("z", "c"), ("y", "x")
    every = vert + feat
    in_specs = (
        P(feat, vert),
        P(),
        P(),
        P(),
        P(every, None, None),
        P(every),
        P(every),
        P(every),
        P(vert, None, None),
        P(every, None),
    )
    out_specs = (P(every, None), P(feat, vert), P(), P(), P())
    return jax.shard_map(local, mesh=grid, in_specs=in_specs, out_specs=out_specs, check_vma=False)
```

```python
import functools

import jax
import jax.numpy as jnp
from jax import lax
from jax.experimental import pallas as pl
from jax.experimental.pallas import tpu as pltpu
from jax.sharding import Mesh
from jax.sharding import PartitionSpec as P

X, Y, Z, C = 4, 8, 12, 2
MEMBERS = X * Y
SLABS = Z * C
F = 128
H = 256
TILE = 128
SLOTS = 2
OWN = 64
AWAY = SLABS * SLOTS
TABLE = OWN + AWAY
ROWS = F // MEMBERS
BPD = 96
OWNED = 2 * TILE
COLS = TABLE * TILE
OWN_COLS = OWN * TILE
AWAY_COLS = AWAY * TILE
WIDE = 2 * H + TILE
PER = H // MEMBERS
EXTRA = X * 2 * H + TILE
GROUP = 8
FETCHES = 4
FETCH = BPD // FETCHES
PIECE = COLS // 7

BF = jnp.bfloat16
F32 = jnp.float32
VMEM = pl.BlockSpec(memory_space=pltpu.VMEM)
SMEM = pl.BlockSpec(memory_space=pltpu.SMEM)
HBM = pl.BlockSpec(memory_space=pltpu.HBM)
LIMIT = 40 * 1024 * 1024
FULL_LIMIT = 62 * 1024 * 1024


def call(body, ins, outs, scratch=(), places=None, limit=LIMIT):
    return pl.pallas_call(
        body,
        in_specs=ins,
        out_specs=jax.tree.map(lambda _: VMEM, outs) if places is None else places,
        out_shape=outs,
        scratch_shapes=scratch,
        compiler_params=pltpu.CompilerParams(vmem_limit_bytes=limit),
    )


def struct(shape, dtype):
    return jax.ShapeDtypeStruct(shape, dtype)


def lanes(at):
    return pl.ds(pl.multiple_of(at * TILE, TILE), TILE)


def pick_kernel(send, feats, out, same):
    same[...] = feats[...]
    for slab in range(SLABS):
        for slot in range(SLOTS):
            tile = feats[:, lanes(send[slot, slab])]
            out[slab, slot * ROWS : (slot + 1) * ROWS, :] = tile


def table_kernel(feats, incoming, out):
    out[:, :OWN_COLS] = feats[...]
    for slab in range(SLABS):
        for slot in range(SLOTS):
            at = OWN_COLS + (slab * SLOTS + slot) * TILE
            out[:, at : at + TILE] = incoming[slab, slot * ROWS : (slot + 1) * ROWS, :]


def dot(a, b, ca, cb):
    return lax.dot_general(a, b, (((ca,), (cb,)), ((), ())), preferred_element_type=F32)


def iota(shape, axis):
    return lax.broadcasted_iota(jnp.int32, shape, axis)


def layer_kernel(
    src,
    dst,
    count,
    first,
    table_hbm,
    adj_hbm,
    w_self_hbm,
    w_neigh_hbm,
    bias_hbm,
    grad_out_hbm,
    act,
    out_hbm,
    grads,
    out,
    table,
    adj,
    w_self,
    w_neigh,
    bias,
    grad_out,
    gathered,
    terms,
    means,
    sems,
):
    def fetch(k, source, target):
        copy = pltpu.make_async_copy(source, target, sems.at[k])
        copy.start()
        return copy

    get_table = fetch(0, table_hbm, table)
    get_adj = [
        fetch(1 + k, adj_hbm.at[pl.ds(k * FETCH, FETCH)], adj.at[pl.ds(k * FETCH, FETCH)])
        for k in range(FETCHES)
    ]
    rest = [
        fetch(1 + FETCHES + k, source, target)
        for k, (source, target) in enumerate(
            (
                (w_self_hbm, w_self),
                (w_neigh_hbm, w_neigh),
                (bias_hbm, bias),
                (grad_out_hbm, grad_out),
            )
        )
    ]

    row, col = iota((F, F), 0), iota((F, F), 1)

    x_of, y_of = (col // ROWS) % X, col // (ROWS * X)
    order = (row == x_of * (Y * ROWS) + y_of * ROWS + col % ROWS).astype(F32).astype(BF)
    live = count[0]
    gathered[...] = jnp.zeros_like(gathered)
    terms[...] = jnp.zeros_like(terms)
    ones = jnp.ones((8, GROUP * TILE), BF)
    get_table.wait()

    def forward(g, carry):
        left, right = [], []
        for j in range(GROUP):
            b = g * GROUP + j
            left.append(table[:, lanes(src[b])])
            block = adj[b]
            alive = b < live
            halves = []
            for t in range(2):
                keep = jnp.where(jnp.logical_and(alive, dst[b] == t), 1.0, 0.0)
                halves.append(block * jnp.full((TILE, TILE), keep, F32).astype(BF))
            right.append(jnp.concatenate(halves, axis=0))
        lhs = jnp.concatenate([jnp.concatenate(left, axis=1), ones], axis=0)
        gathered[...] += dot(lhs, jnp.concatenate(right, axis=1), 1, 1)
        return carry

    groups = lax.div(live + (GROUP - 1), GROUP)
    per = FETCH // GROUP
    for k in range(FETCHES):
        get_adj[k].wait()
        lax.fori_loop(k * per, jnp.minimum(groups, (k + 1) * per), forward, 0)
    for copy in rest:
        copy.wait()
    degree = gathered[F : F + 1, :]
    mean = (gathered[:F, :] / degree).astype(BF)
    start = pl.multiple_of(first[0], OWNED)
    own = table[:, pl.ds(start, OWNED)]
    pre = dot(own, w_self[...], 0, 0) + dot(mean, w_neigh[...], 0, 0) + bias[...]
    sig = jax.nn.sigmoid(pre)
    act[...] = (pre * sig).astype(BF)
    grad_pre = (grad_out[...].astype(F32) * sig * (1.0 + pre * (1.0 - sig))).astype(BF)

    for k, value in enumerate((own, mean)):
        part = dot(value, grad_pre, 1, 0)
        for m in range(MEMBERS):
            grads[m, :, k * H : (k + 1) * H] = part[m * ROWS : (m + 1) * ROWS, :]
    part_bias = jnp.sum(grad_pre.astype(F32), axis=0, keepdims=True)
    mine = iota((F, H), 1) // PER == iota((F, H), 0) // ROWS
    squeeze = (iota((H, TILE), 0) % PER == iota((H, TILE), 1)).astype(F32).astype(BF)
    spread, rest_of = jnp.zeros((F, TILE), F32), part_bias
    for _ in range(3):
        high = rest_of.astype(BF).astype(F32)
        rest_of = rest_of - high
        spread += dot(jnp.where(mine, high, 0.0).astype(BF), squeeze, 1, 0)
    for m in range(MEMBERS):
        grads[m, :, 2 * H :] = spread[m * ROWS : (m + 1) * ROWS, :]

    def reorder(value):
        return dot(order, value, 1, 0).astype(BF)

    from_self = dot(reorder(w_self[...]), grad_pre, 1, 1)
    grad_mean = (dot(reorder(w_neigh[...]), grad_pre, 1, 1) / degree).astype(BF)
    means[0] = grad_mean[:, :TILE]
    means[1] = grad_mean[:, TILE:]
    means[2] = jnp.zeros((F, TILE), BF)
    terms[:, pl.ds(start, OWNED)] = from_self

    def backward(g, carry):
        for j in range(GROUP):
            b = g * GROUP + j
            value = means[jnp.where(b < live, dst[b], 2)]
            terms[:, lanes(src[b])] += dot(value, adj[b], 1, 0)
        return carry

    lax.fori_loop(0, groups, backward, 0)

    puts = []
    for n in range(0, COLS, PIECE):
        at = slice(n, n + PIECE)
        out[:, at] = terms[:, at].astype(BF)
        put = pltpu.make_async_copy(out.at[:, at], out_hbm.at[:, at], sems.at[n // PIECE])
        put.start()
        puts.append(put)
    for put in puts:
        put.wait()


def feat_sum_kernel(parts, out):
    total = sum(parts[m] for m in range(MEMBERS))
    for k in range(SLABS):
        out[k] = total


def vert_sum_kernel(parts, out):
    out[...] = sum(parts[k] for k in range(SLABS))


def join_kernel(terms, grads, out):
    for y in range(Y):
        out[y, :, :COLS] = terms[y * ROWS : (y + 1) * ROWS, :]
    bias = grads[0, :, 2 * H :]
    for x in range(1, X):
        bias += pltpu.roll(grads[x, :, 2 * H :], x * PER, 1)
    bias = bias.astype(BF)
    for x in range(X):
        value = grads[x, :, : 2 * H].astype(BF)
        at = COLS + x * 2 * H
        for y in range(Y):
            out[y, :, at : at + 2 * H] = value
    for y in range(Y):
        out[y, :, COLS + X * 2 * H :] = bias


def sum_kernel(parts, own, away, extra):
    def total(at, width):
        return sum(parts[y, :, at : at + width].astype(F32) for y in range(Y))

    for at in range(0, OWN_COLS, 1024):
        own[:, at : at + 1024] = total(at, 1024)
    for slab in range(SLABS):
        for slot in range(SLOTS):
            tile = total(OWN_COLS + (slab * SLOTS + slot) * TILE, TILE)
            away[slab, slot * ROWS : (slot + 1) * ROWS, :] = tile.astype(BF)
    for y in range(Y):
        extra[y] = parts[y, :, COLS:]


def land_kernel(send, own, back, extra, out, grad_self, grad_neigh, grad_bias):
    out[...] = own[...]
    for slab in range(SLABS):
        for slot in range(SLOTS):
            tile = back[slab, slot * ROWS : (slot + 1) * ROWS, :].astype(F32)
            out[:, lanes(send[slot, slab])] += tile
    for y in range(Y):
        for x in range(X):
            at = (y * X + x) * ROWS
            value = extra[y, :, x * 2 * H : (x + 1) * 2 * H].astype(F32)
            grad_self[at : at + ROWS, :] = value[:, :H]
            grad_neigh[at : at + ROWS, :] = value[:, H:]
    each = X * PER
    for half in range(H // TILE):
        first = half * (TILE // each)
        value = extra[first, :, X * 2 * H :].astype(F32)
        for k in range(1, TILE // each):
            value += pltpu.roll(extra[first + k, :, X * 2 * H :].astype(F32), k * each, 1)
        grad_bias[:, half * TILE : (half + 1) * TILE] = value[:1]


def local(
    node_feats,
    w_self,
    w_neigh,
    out_bias,
    adjacency,
    block_dst,
    block_src,
    block_count,
    send_list,
    grad_out,
):
    vert, feat = ("z", "c"), ("y", "x")
    send = jnp.swapaxes(send_list[0], 0, 1)
    first = (lax.axis_index(feat) * OWNED).astype(jnp.int32).reshape(1)
    outgoing, feats = call(
        pick_kernel,
        [SMEM, VMEM],
        (struct((SLABS, SLOTS * ROWS, TILE), BF), struct((ROWS, OWN_COLS), BF)),
    )(send, node_feats)
    incoming = lax.all_to_all(outgoing, vert, 0, 0, tiled=True)
    table = call(table_kernel, [VMEM, VMEM], struct((ROWS, COLS), BF))(feats, incoming)
    table = lax.all_gather(table, "x", axis=0, tiled=True)
    table = lax.all_gather(table, "y", axis=0, tiled=True)
    activated, terms, grads = call(
        layer_kernel,
        [SMEM] * 4 + [HBM] * 6,
        (struct((OWNED, H), BF), struct((F, COLS), BF), struct((MEMBERS, ROWS, WIDE), F32)),
        (
            pltpu.VMEM((F, COLS), BF),
            pltpu.VMEM((F, COLS), BF),
            pltpu.VMEM((BPD, TILE, TILE), BF),
            pltpu.VMEM((F, H), BF),
            pltpu.VMEM((F, H), BF),
            pltpu.VMEM((1, H), F32),
            pltpu.VMEM((OWNED, H), BF),
            pltpu.VMEM((F + 8, OWNED), F32),
            pltpu.VMEM((F, COLS), F32),
            pltpu.VMEM((3, F, TILE), BF),
            pltpu.SemaphoreType.DMA((1 + FETCHES + 4,)),
        ),
        (VMEM, HBM, VMEM),
        FULL_LIMIT,
    )(
        block_src,
        block_dst,
        block_count,
        first,
        table,
        adjacency,
        w_self,
        w_neigh,
        out_bias.reshape(1, H),
        grad_out,
    )
    terms = lax.psum_scatter(terms, "x", scatter_dimension=0, tiled=True)
    grads = lax.all_to_all(grads, feat, 0, 0, tiled=True)
    grads = call(feat_sum_kernel, [VMEM], struct((SLABS, ROWS, WIDE), F32))(grads)
    grads = lax.all_to_all(grads, vert, 0, 0, tiled=True)
    grads = call(vert_sum_kernel, [VMEM], struct((ROWS, WIDE), F32))(grads)
    grads = lax.all_gather(grads, "x", axis=0, tiled=False)
    terms, grads = lax.optimization_barrier((terms, grads))
    terms = call(join_kernel, [VMEM, VMEM], struct((Y, ROWS, COLS + EXTRA), BF))(terms, grads)
    terms = lax.all_to_all(terms, "y", 0, 0, tiled=True)
    own, away, extra = call(
        sum_kernel,
        [VMEM],
        (
            struct((ROWS, OWN_COLS), F32),
            struct((SLABS, SLOTS * ROWS, TILE), BF),
            struct((Y, ROWS, EXTRA), BF),
        ),
    )(terms)
    back = lax.all_to_all(away, vert, 0, 0, tiled=True)
    grad_feats, grad_self, grad_neigh, grad_bias = call(
        land_kernel,
        [SMEM, VMEM, VMEM, VMEM],
        (
            struct((ROWS, OWN_COLS), F32),
            struct((F, H), F32),
            struct((F, H), F32),
            struct((1, H), F32),
        ),
    )(send, own, back, extra)
    return activated, grad_feats, grad_self, grad_neigh, grad_bias.reshape(H)


def solution(mesh):
    grid = Mesh(mesh.devices.reshape(Z, C, Y, X), ("z", "c", "y", "x"))
    vert, feat = ("z", "c"), ("y", "x")
    every = vert + feat
    in_specs = (
        P(feat, vert),
        P(),
        P(),
        P(),
        P(every, None, None),
        P(every),
        P(every),
        P(every),
        P(vert, None, None),
        P(every, None),
    )
    out_specs = (P(every, None), P(feat, vert), P(), P(), P())
    return jax.shard_map(local, mesh=grid, in_specs=in_specs, out_specs=out_specs, check_vma=False)
```

```python
import functools

import jax
import jax.numpy as jnp
from jax import lax
from jax.experimental import pallas as pl
from jax.experimental.pallas import tpu as pltpu
from jax.sharding import Mesh
from jax.sharding import PartitionSpec as P

X, Y, Z, C = 4, 8, 12, 2
MEMBERS = X * Y
SLABS = Z * C
F = 128
H = 256
TILE = 128
SLOTS = 2
OWN = 64
AWAY = SLABS * SLOTS
TABLE = OWN + AWAY
ROWS = F // MEMBERS
BPD = 96
OWNED = 2 * TILE
COLS = TABLE * TILE
OWN_COLS = OWN * TILE
AWAY_COLS = AWAY * TILE
WIDE = 2 * H + TILE
PER = H // MEMBERS
GROUP = 8
FETCHES = 4
FETCH = BPD // FETCHES
PIECE = COLS // 7

BF = jnp.bfloat16
F32 = jnp.float32
VMEM = pl.BlockSpec(memory_space=pltpu.VMEM)
SMEM = pl.BlockSpec(memory_space=pltpu.SMEM)
HBM = pl.BlockSpec(memory_space=pltpu.HBM)
LIMIT = 40 * 1024 * 1024
FULL_LIMIT = 62 * 1024 * 1024


def call(body, ins, outs, scratch=(), places=None, limit=LIMIT):
    return pl.pallas_call(
        body,
        in_specs=ins,
        out_specs=jax.tree.map(lambda _: VMEM, outs) if places is None else places,
        out_shape=outs,
        scratch_shapes=scratch,
        compiler_params=pltpu.CompilerParams(vmem_limit_bytes=limit),
    )


def struct(shape, dtype):
    return jax.ShapeDtypeStruct(shape, dtype)


def lanes(at):
    return pl.ds(pl.multiple_of(at * TILE, TILE), TILE)


def pick_kernel(send, feats, out, same):
    same[...] = feats[...]
    for slab in range(SLABS):
        for slot in range(SLOTS):
            tile = feats[:, lanes(send[slot, slab])]
            out[slab, slot * ROWS : (slot + 1) * ROWS, :] = tile


def table_kernel(feats, incoming, out):
    out[:, :OWN_COLS] = feats[...]
    for slab in range(SLABS):
        for slot in range(SLOTS):
            at = OWN_COLS + (slab * SLOTS + slot) * TILE
            out[:, at : at + TILE] = incoming[slab, slot * ROWS : (slot + 1) * ROWS, :]


def dot(a, b, ca, cb):
    return lax.dot_general(a, b, (((ca,), (cb,)), ((), ())), preferred_element_type=F32)


def iota(shape, axis):
    return lax.broadcasted_iota(jnp.int32, shape, axis)


def layer_kernel(
    src,
    dst,
    count,
    first,
    table_hbm,
    adj_hbm,
    w_self_hbm,
    w_neigh_hbm,
    bias_hbm,
    grad_out_hbm,
    act,
    out_hbm,
    grads,
    out,
    table,
    adj,
    w_self,
    w_neigh,
    bias,
    grad_out,
    gathered,
    terms,
    means,
    sems,
):
    def fetch(k, source, target):
        return pltpu.make_async_copy(source, target, sems.at[k])

    get_table = fetch(0, table_hbm, table)
    get_adj = [
        fetch(1 + k, adj_hbm.at[pl.ds(k * FETCH, FETCH)], adj.at[pl.ds(k * FETCH, FETCH)])
        for k in range(FETCHES)
    ]
    rest = [
        fetch(1 + FETCHES + k, source, target)
        for k, (source, target) in enumerate(
            (
                (w_self_hbm, w_self),
                (w_neigh_hbm, w_neigh),
                (bias_hbm, bias),
                (grad_out_hbm, grad_out),
            )
        )
    ]

    get_table.start()
    get_adj[0].start()
    row, col = iota((F, F), 0), iota((F, F), 1)

    x_of, y_of = (col // ROWS) % X, col // (ROWS * X)
    order = (row == x_of * (Y * ROWS) + y_of * ROWS + col % ROWS).astype(F32).astype(BF)
    live = count[0]
    gathered[...] = jnp.zeros_like(gathered)
    terms[...] = jnp.zeros_like(terms)
    ones = jnp.ones((8, GROUP * TILE), BF)
    get_table.wait()
    for copy in get_adj[1:] + rest:
        copy.start()

    def forward(g, carry):
        left, right = [], []
        for j in range(GROUP):
            b = g * GROUP + j
            left.append(table[:, lanes(src[b])])
            block = adj[b]
            alive = b < live
            halves = []
            for t in range(2):
                keep = jnp.where(jnp.logical_and(alive, dst[b] == t), 1.0, 0.0)
                halves.append(block * jnp.full((TILE, TILE), keep, F32).astype(BF))
            right.append(jnp.concatenate(halves, axis=0))
        lhs = jnp.concatenate([jnp.concatenate(left, axis=1), ones], axis=0)
        gathered[...] += dot(lhs, jnp.concatenate(right, axis=1), 1, 1)
        return carry

    groups = lax.div(live + (GROUP - 1), GROUP)
    per = FETCH // GROUP
    for k in range(FETCHES):
        get_adj[k].wait()
        lax.fori_loop(k * per, jnp.minimum(groups, (k + 1) * per), forward, 0)
    for copy in rest:
        copy.wait()
    degree = gathered[F : F + 1, :]
    mean = (gathered[:F, :] / degree).astype(BF)
    start = pl.multiple_of(first[0], OWNED)
    own = table[:, pl.ds(start, OWNED)]
    pre = dot(own, w_self[...], 0, 0) + dot(mean, w_neigh[...], 0, 0) + bias[...]
    sig = jax.nn.sigmoid(pre)
    act[...] = (pre * sig).astype(BF)
    grad_pre = (grad_out[...].astype(F32) * sig * (1.0 + pre * (1.0 - sig))).astype(BF)

    for k, value in enumerate((own, mean)):
        part = dot(value, grad_pre, 1, 0)
        for m in range(MEMBERS):
            grads[m, :, k * H : (k + 1) * H] = part[m * ROWS : (m + 1) * ROWS, :]
    part_bias = jnp.sum(grad_pre.astype(F32), axis=0, keepdims=True)
    mine = iota((F, H), 1) // PER == iota((F, H), 0) // ROWS
    squeeze = (iota((H, TILE), 0) % PER == iota((H, TILE), 1)).astype(F32).astype(BF)
    spread, rest_of = jnp.zeros((F, TILE), F32), part_bias
    for _ in range(3):
        high = rest_of.astype(BF).astype(F32)
        rest_of = rest_of - high
        spread += dot(jnp.where(mine, high, 0.0).astype(BF), squeeze, 1, 0)
    for m in range(MEMBERS):
        grads[m, :, 2 * H :] = spread[m * ROWS : (m + 1) * ROWS, :]

    def reorder(value):
        return dot(order, value, 1, 0).astype(BF)

    from_self = dot(reorder(w_self[...]), grad_pre, 1, 1)
    grad_mean = (dot(reorder(w_neigh[...]), grad_pre, 1, 1) / degree).astype(BF)
    means[0] = grad_mean[:, :TILE]
    means[1] = grad_mean[:, TILE:]
    means[2] = jnp.zeros((F, TILE), BF)
    terms[:, pl.ds(start, OWNED)] = from_self

    def backward(g, carry):
        for j in range(GROUP):
            b = g * GROUP + j
            value = means[jnp.where(b < live, dst[b], 2)]
            terms[:, lanes(src[b])] += dot(value, adj[b], 1, 0)
        return carry

    lax.fori_loop(0, groups, backward, 0)

    puts = []
    for n in range(0, COLS, PIECE):
        at = slice(n, n + PIECE)
        out[:, at] = terms[:, at].astype(BF)
        put = pltpu.make_async_copy(out.at[:, at], out_hbm.at[:, at], sems.at[n // PIECE])
        put.start()
        puts.append(put)
    for put in puts:
        put.wait()


def feat_sum_kernel(parts, out):
    total = sum(parts[m] for m in range(MEMBERS))
    for k in range(SLABS):
        out[k] = total


def vert_sum_kernel(parts, out):
    out[...] = sum(parts[k] for k in range(SLABS))


def join_kernel(terms, grads, out):
    for y in range(Y):
        out[y, :, :COLS] = terms[y * ROWS : (y + 1) * ROWS, :]
    value = grads[...].astype(BF)
    for y in range(Y):
        out[y, :, COLS:] = value


def sum_kernel(parts, own, away, extra):
    def total(at, width):
        return sum(parts[y, :, at : at + width].astype(F32) for y in range(Y))

    for at in range(0, OWN_COLS, 1024):
        own[:, at : at + 1024] = total(at, 1024)
    for slab in range(SLABS):
        for slot in range(SLOTS):
            tile = total(OWN_COLS + (slab * SLOTS + slot) * TILE, TILE)
            away[slab, slot * ROWS : (slot + 1) * ROWS, :] = tile.astype(BF)
    for y in range(Y):
        extra[y] = parts[y, :, COLS:].astype(F32)


def land_kernel(
    send, place, own, back, extra0, extra1, extra2, extra3, out, grad_self, grad_neigh, grad_bias, held
):
    out[...] = own[...]
    for slab in range(SLABS):
        for slot in range(SLOTS):
            tile = back[slab, slot * ROWS : (slot + 1) * ROWS, :].astype(F32)
            out[:, lanes(send[slot, slab])] += tile
    for shift, extra in enumerate((extra0, extra1, extra2, extra3)):
        held[lax.rem(place[0] + (X - shift), X)] = extra[...]
    bias = [jnp.zeros((1, TILE), F32) for _ in range(H // TILE)]
    for y in range(Y):
        value = jnp.concatenate([held[x, y, :, : 2 * H] for x in range(X)], axis=0)
        at = y * X * ROWS
        grad_self[at : at + X * ROWS, :] = value[:, :H]
        grad_neigh[at : at + X * ROWS, :] = value[:, H:]
        for x in range(X):
            half, lane = divmod((y * X + x) * PER, TILE)
            bias[half] += pltpu.roll(held[x, y, :, 2 * H :], lane, 1)[:1]
    for half in range(H // TILE):
        grad_bias[:, half * TILE : (half + 1) * TILE] = bias[half]


def local(
    node_feats,
    w_self,
    w_neigh,
    out_bias,
    adjacency,
    block_dst,
    block_src,
    block_count,
    send_list,
    grad_out,
):
    vert, feat = ("z", "c"), ("y", "x")
    send = jnp.swapaxes(send_list[0], 0, 1)
    first = (lax.axis_index(feat) * OWNED).astype(jnp.int32).reshape(1)
    outgoing, feats = call(
        pick_kernel,
        [SMEM, VMEM],
        (struct((SLABS, SLOTS * ROWS, TILE), BF), struct((ROWS, OWN_COLS), BF)),
    )(send, node_feats)
    incoming = lax.all_to_all(outgoing, vert, 0, 0, tiled=True)
    table = call(table_kernel, [VMEM, VMEM], struct((ROWS, COLS), BF))(feats, incoming)
    table = lax.all_gather(table, "x", axis=0, tiled=True)
    table = lax.all_gather(table, "y", axis=0, tiled=True)
    activated, terms, grads = call(
        layer_kernel,
        [SMEM] * 4 + [HBM] * 6,
        (struct((OWNED, H), BF), struct((F, COLS), BF), struct((MEMBERS, ROWS, WIDE), F32)),
        (
            pltpu.VMEM((F, COLS), BF),
            pltpu.VMEM((F, COLS), BF),
            pltpu.VMEM((BPD, TILE, TILE), BF),
            pltpu.VMEM((F, H), BF),
            pltpu.VMEM((F, H), BF),
            pltpu.VMEM((1, H), F32),
            pltpu.VMEM((OWNED, H), BF),
            pltpu.VMEM((F + 8, OWNED), F32),
            pltpu.VMEM((F, COLS), F32),
            pltpu.VMEM((3, F, TILE), BF),
            pltpu.SemaphoreType.DMA((1 + FETCHES + 4,)),
        ),
        (VMEM, HBM, VMEM),
        FULL_LIMIT,
    )(
        block_src,
        block_dst,
        block_count,
        first,
        table,
        adjacency,
        w_self,
        w_neigh,
        out_bias.reshape(1, H),
        grad_out,
    )
    terms = lax.psum_scatter(terms, "x", scatter_dimension=0, tiled=True)
    grads = lax.all_to_all(grads, feat, 0, 0, tiled=True)
    grads = call(feat_sum_kernel, [VMEM], struct((SLABS, ROWS, WIDE), F32))(grads)
    grads = lax.all_to_all(grads, vert, 0, 0, tiled=True)
    grads = call(vert_sum_kernel, [VMEM], struct((ROWS, WIDE), F32))(grads)
    terms, grads = lax.optimization_barrier((terms, grads))
    terms = call(join_kernel, [VMEM, VMEM], struct((Y, ROWS, COLS + WIDE), BF))(terms, grads)
    terms = lax.all_to_all(terms, "y", 0, 0, tiled=True)
    own, away, extra = call(
        sum_kernel,
        [VMEM],
        (
            struct((ROWS, OWN_COLS), F32),
            struct((SLABS, SLOTS * ROWS, TILE), BF),
            struct((Y, ROWS, WIDE), F32),
        ),
    )(terms)
    others = [
        lax.ppermute(extra, "x", [(k, (k + shift) % X) for k in range(X)]) for shift in range(1, X)
    ]
    back = lax.all_to_all(away, vert, 0, 0, tiled=True)
    place = lax.axis_index("x").astype(jnp.int32).reshape(1)
    grad_feats, grad_self, grad_neigh, grad_bias = call(
        land_kernel,
        [SMEM, SMEM] + [VMEM] * 6,
        (
            struct((ROWS, OWN_COLS), F32),
            struct((F, H), F32),
            struct((F, H), F32),
            struct((1, H), F32),
        ),
        (pltpu.VMEM((X, Y, ROWS, WIDE), F32),),
    )(send, place, own, back, extra, *others)
    return activated, grad_feats, grad_self, grad_neigh, grad_bias.reshape(H)


def solution(mesh):
    grid = Mesh(mesh.devices.reshape(Z, C, Y, X), ("z", "c", "y", "x"))
    vert, feat = ("z", "c"), ("y", "x")
    every = vert + feat
    in_specs = (
        P(feat, vert),
        P(),
        P(),
        P(),
        P(every, None, None),
        P(every),
        P(every),
        P(every),
        P(vert, None, None),
        P(every, None),
    )
    out_specs = (P(every, None), P(feat, vert), P(), P(), P())
    return jax.shard_map(local, mesh=grid, in_specs=in_specs, out_specs=out_specs, check_vma=False)
```

```python
import functools

import jax
import jax.numpy as jnp
from jax import lax
from jax.experimental import pallas as pl
from jax.experimental.pallas import tpu as pltpu
from jax.sharding import Mesh
from jax.sharding import PartitionSpec as P

X, Y, Z, C = 4, 8, 12, 2
MEMBERS = X * Y
SLABS = Z * C
F = 128
H = 256
TILE = 128
SLOTS = 2
OWN = 64
AWAY = SLABS * SLOTS
TABLE = OWN + AWAY
ROWS = F // MEMBERS
BPD = 96
OWNED = 2 * TILE
COLS = TABLE * TILE
OWN_COLS = OWN * TILE
AWAY_COLS = AWAY * TILE
PART = 16
CHUNK = 2 * PART + 8
TOTAL = PART + 8
PER = H // MEMBERS
EXTRA = X * PART // ROWS * TILE + TILE
GROUP = 8
FETCHES = 4
FETCH = BPD // FETCHES
PIECE = COLS // 7

BF = jnp.bfloat16
F32 = jnp.float32
VMEM = pl.BlockSpec(memory_space=pltpu.VMEM)
SMEM = pl.BlockSpec(memory_space=pltpu.SMEM)
HBM = pl.BlockSpec(memory_space=pltpu.HBM)
LIMIT = 40 * 1024 * 1024
FULL_LIMIT = 62 * 1024 * 1024


def call(body, ins, outs, scratch=(), places=None, limit=LIMIT):
    return pl.pallas_call(
        body,
        in_specs=ins,
        out_specs=jax.tree.map(lambda _: VMEM, outs) if places is None else places,
        out_shape=outs,
        scratch_shapes=scratch,
        compiler_params=pltpu.CompilerParams(vmem_limit_bytes=limit),
    )


def struct(shape, dtype):
    return jax.ShapeDtypeStruct(shape, dtype)


def lanes(at):
    return pl.ds(pl.multiple_of(at * TILE, TILE), TILE)


def pick_kernel(send, feats, out, same):
    same[...] = feats[...]
    for slab in range(SLABS):
        for slot in range(SLOTS):
            tile = feats[:, lanes(send[slot, slab])]
            out[slab, slot * ROWS : (slot + 1) * ROWS, :] = tile


def table_kernel(feats, incoming, out):
    out[:, :OWN_COLS] = feats[...]
    for slab in range(SLABS):
        for slot in range(SLOTS):
            at = OWN_COLS + (slab * SLOTS + slot) * TILE
            out[:, at : at + TILE] = incoming[slab, slot * ROWS : (slot + 1) * ROWS, :]


def dot(a, b, ca, cb):
    return lax.dot_general(a, b, (((ca,), (cb,)), ((), ())), preferred_element_type=F32)


def split(value):
    high = value.astype(BF)
    return high, (value - high.astype(F32)).astype(BF)


def gather_parts(parts, count):
    whole = sum(parts[k, : 2 * PART, :].astype(F32) for k in range(count))
    bias = sum(parts[k, 2 * PART :, :].astype(F32) for k in range(count))
    return whole[:PART] + whole[PART:], bias[:4] + bias[4:]


def iota(shape, axis):
    return lax.broadcasted_iota(jnp.int32, shape, axis)


def layer_kernel(
    src,
    dst,
    count,
    first,
    table_hbm,
    adj_hbm,
    w_self_hbm,
    w_neigh_hbm,
    bias_hbm,
    grad_out_hbm,
    act,
    out_hbm,
    grads,
    out,
    table,
    adj,
    w_self,
    w_neigh,
    bias,
    grad_out,
    gathered,
    terms,
    means,
    sems,
):
    def fetch(k, source, target):
        return pltpu.make_async_copy(source, target, sems.at[k])

    get_table = fetch(0, table_hbm, table)
    get_adj = [
        fetch(1 + k, adj_hbm.at[pl.ds(k * FETCH, FETCH)], adj.at[pl.ds(k * FETCH, FETCH)])
        for k in range(FETCHES)
    ]
    rest = [
        fetch(1 + FETCHES + k, source, target)
        for k, (source, target) in enumerate(
            (
                (w_self_hbm, w_self),
                (w_neigh_hbm, w_neigh),
                (bias_hbm, bias),
                (grad_out_hbm, grad_out),
            )
        )
    ]

    get_table.start()
    get_adj[0].start()
    row, col = iota((F, F), 0), iota((F, F), 1)

    x_of, y_of = (col // ROWS) % X, col // (ROWS * X)
    order = (row == x_of * (Y * ROWS) + y_of * ROWS + col % ROWS).astype(F32).astype(BF)
    live = count[0]
    gathered[...] = jnp.zeros_like(gathered)
    terms[...] = jnp.zeros_like(terms)
    ones = jnp.ones((8, GROUP * TILE), BF)
    get_table.wait()
    for copy in get_adj[1:] + rest:
        copy.start()

    def forward(g, carry):
        left, right = [], []
        for j in range(GROUP):
            b = g * GROUP + j
            left.append(table[:, lanes(src[b])])
            block = adj[b]
            alive = b < live
            halves = []
            for t in range(2):
                keep = jnp.where(jnp.logical_and(alive, dst[b] == t), 1.0, 0.0)
                halves.append(block * jnp.full((TILE, TILE), keep, F32).astype(BF))
            right.append(jnp.concatenate(halves, axis=0))
        lhs = jnp.concatenate([jnp.concatenate(left, axis=1), ones], axis=0)
        gathered[...] += dot(lhs, jnp.concatenate(right, axis=1), 1, 1)
        return carry

    groups = lax.div(live + (GROUP - 1), GROUP)
    per = FETCH // GROUP
    for k in range(FETCHES):
        get_adj[k].wait()
        lax.fori_loop(k * per, jnp.minimum(groups, (k + 1) * per), forward, 0)
    for copy in rest:
        copy.wait()
    degree = gathered[F : F + 1, :]
    mean = (gathered[:F, :] / degree).astype(BF)
    start = pl.multiple_of(first[0], OWNED)
    own = table[:, pl.ds(start, OWNED)]
    pre = dot(own, w_self[...], 0, 0) + dot(mean, w_neigh[...], 0, 0) + bias[...]
    sig = jax.nn.sigmoid(pre)
    act[...] = (pre * sig).astype(BF)
    grad_pre = (grad_out[...].astype(F32) * sig * (1.0 + pre * (1.0 - sig))).astype(BF)

    member = 0
    for value in (own, mean):
        both = split(dot(value, grad_pre, 1, 0))
        for k in range(H // TILE):
            for at in range(0, F, PART):
                for half, piece in enumerate(both):
                    grads[member, half * PART : (half + 1) * PART, :] = piece[
                        at : at + PART, k * TILE : (k + 1) * TILE
                    ]
                member += 1
    part_bias = jnp.sum(grad_pre.astype(F32), axis=0, keepdims=True)
    mine = iota((MEMBERS, H), 1) // PER == iota((MEMBERS, H), 0)
    squeeze = (iota((H, TILE), 0) % PER == iota((H, TILE), 1)).astype(F32).astype(BF)
    high, low = (
        dot(jnp.where(mine, value.astype(F32), 0.0).astype(BF), squeeze, 1, 0)
        for value in split(part_bias)
    )
    upper = iota((8, TILE), 0) < 4
    for m in range(MEMBERS):
        grads[m, 2 * PART :, :] = jnp.where(upper, high[m : m + 1], low[m : m + 1]).astype(BF)

    def reorder(value):
        return dot(order, value, 1, 0).astype(BF)

    from_self = dot(reorder(w_self[...]), grad_pre, 1, 1)
    grad_mean = (dot(reorder(w_neigh[...]), grad_pre, 1, 1) / degree).astype(BF)
    means[0] = grad_mean[:, :TILE]
    means[1] = grad_mean[:, TILE:]
    means[2] = jnp.zeros((F, TILE), BF)
    terms[:, pl.ds(start, OWNED)] = from_self

    def backward(g, carry):
        for j in range(GROUP):
            b = g * GROUP + j
            value = means[jnp.where(b < live, dst[b], 2)]
            terms[:, lanes(src[b])] += dot(value, adj[b], 1, 0)
        return carry

    lax.fori_loop(0, groups, backward, 0)

    puts = []
    for n in range(0, COLS, PIECE):
        at = slice(n, n + PIECE)
        out[:, at] = terms[:, at].astype(BF)
        put = pltpu.make_async_copy(out.at[:, at], out_hbm.at[:, at], sems.at[n // PIECE])
        put.start()
        puts.append(put)
    for put in puts:
        put.wait()


def feat_sum_kernel(parts, out):
    whole, bias = gather_parts(parts, MEMBERS)
    high, low = split(whole)
    pair = [value.astype(F32) for value in split(bias)]
    ends = jnp.concatenate(pair, axis=0).astype(BF)
    for k in range(SLABS):
        out[k, :PART, :] = high
        out[k, PART : 2 * PART, :] = low
        out[k, 2 * PART :, :] = ends


def vert_sum_kernel(parts, out):
    whole, bias = gather_parts(parts, SLABS)
    out[:PART, :] = whole
    out[PART:, :] = jnp.concatenate([bias, bias], axis=0)


def join_kernel(terms, grads, out):
    for y in range(Y):
        out[y, :, :COLS] = terms[y * ROWS : (y + 1) * ROWS, :]
    at = COLS
    for x in range(X):
        for k in range(0, PART, ROWS):
            value = grads[x, k : k + ROWS, :].astype(BF)
            for y in range(Y):
                out[y, :, at : at + TILE] = value
            at += TILE
    bias = grads[0, PART : PART + ROWS, :]
    for x in range(1, X):
        bias += pltpu.roll(grads[x, PART : PART + ROWS, :], x * PER, 1)
    for y in range(Y):
        out[y, :, at:] = bias.astype(BF)


def sum_kernel(parts, own, away, extra):
    def total(at, width):
        return sum(parts[y, :, at : at + width].astype(F32) for y in range(Y))

    for at in range(0, OWN_COLS, 1024):
        own[:, at : at + 1024] = total(at, 1024)
    for slab in range(SLABS):
        for slot in range(SLOTS):
            tile = total(OWN_COLS + (slab * SLOTS + slot) * TILE, TILE)
            away[slab, slot * ROWS : (slot + 1) * ROWS, :] = tile.astype(BF)
    for y in range(Y):
        extra[y] = parts[y, :, COLS:]


def land_kernel(send, own, back, extra, out, grad_self, grad_neigh, grad_bias):
    out[...] = own[...]
    for slab in range(SLABS):
        for slot in range(SLOTS):
            tile = back[slab, slot * ROWS : (slot + 1) * ROWS, :].astype(F32)
            out[:, lanes(send[slot, slab])] += tile
    pieces = X * PART // ROWS
    for y in range(Y):
        block, at = divmod(y * X * PART, F)
        target = (grad_self, grad_neigh)[block // 2]
        lane = (block % 2) * TILE
        for k in range(0, pieces, 2):
            value = jnp.concatenate(
                [extra[y, :, j * TILE : (j + 1) * TILE].astype(F32) for j in (k, k + 1)], axis=0
            )
            target[at + k * ROWS : at + (k + 2) * ROWS, lane : lane + TILE] = value
    each = X * PER
    for half in range(H // TILE):
        first = half * (TILE // each)
        value = extra[first, :, pieces * TILE :].astype(F32)
        for k in range(1, TILE // each):
            value += pltpu.roll(extra[first + k, :, pieces * TILE :].astype(F32), k * each, 1)
        grad_bias[:, half * TILE : (half + 1) * TILE] = value[:1]


def local(
    node_feats,
    w_self,
    w_neigh,
    out_bias,
    adjacency,
    block_dst,
    block_src,
    block_count,
    send_list,
    grad_out,
):
    vert, feat = ("z", "c"), ("y", "x")
    send = jnp.swapaxes(send_list[0], 0, 1)
    first = (lax.axis_index(feat) * OWNED).astype(jnp.int32).reshape(1)
    outgoing, feats = call(
        pick_kernel,
        [SMEM, VMEM],
        (struct((SLABS, SLOTS * ROWS, TILE), BF), struct((ROWS, OWN_COLS), BF)),
    )(send, node_feats)
    incoming = lax.all_to_all(outgoing, vert, 0, 0, tiled=True)
    table = call(table_kernel, [VMEM, VMEM], struct((ROWS, COLS), BF))(feats, incoming)
    table = lax.all_gather(table, "x", axis=0, tiled=True)
    table = lax.all_gather(table, "y", axis=0, tiled=True)
    activated, terms, grads = call(
        layer_kernel,
        [SMEM] * 4 + [HBM] * 6,
        (struct((OWNED, H), BF), struct((F, COLS), BF), struct((MEMBERS, CHUNK, TILE), BF)),
        (
            pltpu.VMEM((F, COLS), BF),
            pltpu.VMEM((F, COLS), BF),
            pltpu.VMEM((BPD, TILE, TILE), BF),
            pltpu.VMEM((F, H), BF),
            pltpu.VMEM((F, H), BF),
            pltpu.VMEM((1, H), F32),
            pltpu.VMEM((OWNED, H), BF),
            pltpu.VMEM((F + 8, OWNED), F32),
            pltpu.VMEM((F, COLS), F32),
            pltpu.VMEM((3, F, TILE), BF),
            pltpu.SemaphoreType.DMA((1 + FETCHES + 4,)),
        ),
        (VMEM, HBM, VMEM),
        FULL_LIMIT,
    )(
        block_src,
        block_dst,
        block_count,
        first,
        table,
        adjacency,
        w_self,
        w_neigh,
        out_bias.reshape(1, H),
        grad_out,
    )
    terms = lax.psum_scatter(terms, "x", scatter_dimension=0, tiled=True)
    grads = lax.all_to_all(grads, feat, 0, 0, tiled=True)
    grads = call(feat_sum_kernel, [VMEM], struct((SLABS, CHUNK, TILE), BF))(grads)
    grads = lax.all_to_all(grads, vert, 0, 0, tiled=True)
    grads = call(vert_sum_kernel, [VMEM], struct((TOTAL, TILE), F32))(grads)
    grads = lax.all_gather(grads, "x", axis=0, tiled=False)
    terms, grads = lax.optimization_barrier((terms, grads))
    terms = call(join_kernel, [VMEM, VMEM], struct((Y, ROWS, COLS + EXTRA), BF))(terms, grads)
    terms = lax.all_to_all(terms, "y", 0, 0, tiled=True)
    own, away, extra = call(
        sum_kernel,
        [VMEM],
        (
            struct((ROWS, OWN_COLS), F32),
            struct((SLABS, SLOTS * ROWS, TILE), BF),
            struct((Y, ROWS, EXTRA), BF),
        ),
    )(terms)
    back = lax.all_to_all(away, vert, 0, 0, tiled=True)
    grad_feats, grad_self, grad_neigh, grad_bias = call(
        land_kernel,
        [SMEM, VMEM, VMEM, VMEM],
        (
            struct((ROWS, OWN_COLS), F32),
            struct((F, H), F32),
            struct((F, H), F32),
            struct((1, H), F32),
        ),
    )(send, own, back, extra)
    return activated, grad_feats, grad_self, grad_neigh, grad_bias.reshape(H)


def solution(mesh):
    grid = Mesh(mesh.devices.reshape(Z, C, Y, X), ("z", "c", "y", "x"))
    vert, feat = ("z", "c"), ("y", "x")
    every = vert + feat
    in_specs = (
        P(feat, vert),
        P(),
        P(),
        P(),
        P(every, None, None),
        P(every),
        P(every),
        P(every),
        P(vert, None, None),
        P(every, None),
    )
    out_specs = (P(every, None), P(feat, vert), P(), P(), P())
    return jax.shard_map(local, mesh=grid, in_specs=in_specs, out_specs=out_specs, check_vma=False)
```

```python
import functools

import jax
import jax.numpy as jnp
from jax import lax
from jax.experimental import pallas as pl
from jax.experimental.pallas import tpu as pltpu
from jax.sharding import Mesh
from jax.sharding import PartitionSpec as P

X, Y, Z, C = 4, 8, 12, 2
MEMBERS = X * Y
SLABS = Z * C
F = 128
H = 256
TILE = 128
SLOTS = 2
OWN = 64
AWAY = SLABS * SLOTS
TABLE = OWN + AWAY
ROWS = F // MEMBERS
BPD = 96
OWNED = 2 * TILE
COLS = TABLE * TILE
OWN_COLS = OWN * TILE
AWAY_COLS = AWAY * TILE
PART = 16
CHUNK = 2 * PART + 8
TOTAL = 72
PER = H // MEMBERS
GROUP = 24
FETCHES = 4
FETCH = BPD // FETCHES
PIECE = COLS // 7

BF = jnp.bfloat16
F32 = jnp.float32
VMEM = pl.BlockSpec(memory_space=pltpu.VMEM)
SMEM = pl.BlockSpec(memory_space=pltpu.SMEM)
HBM = pl.BlockSpec(memory_space=pltpu.HBM)
LIMIT = 40 * 1024 * 1024
FULL_LIMIT = 62 * 1024 * 1024


def call(body, ins, outs, scratch=(), places=None, limit=LIMIT):
    return pl.pallas_call(
        body,
        in_specs=ins,
        out_specs=jax.tree.map(lambda _: VMEM, outs) if places is None else places,
        out_shape=outs,
        scratch_shapes=scratch,
        compiler_params=pltpu.CompilerParams(vmem_limit_bytes=limit),
    )


def struct(shape, dtype):
    return jax.ShapeDtypeStruct(shape, dtype)


def lanes(at):
    return pl.ds(pl.multiple_of(at * TILE, TILE), TILE)


def pick_kernel(send, feats, out, same):
    same[...] = feats[...]
    for slab in range(SLABS):
        for slot in range(SLOTS):
            tile = feats[:, lanes(send[slot, slab])]
            out[slab, slot * ROWS : (slot + 1) * ROWS, :] = tile


def table_kernel(feats, incoming, out):
    out[:, :OWN_COLS] = feats[...]
    for slab in range(SLABS):
        for slot in range(SLOTS):
            at = OWN_COLS + (slab * SLOTS + slot) * TILE
            out[:, at : at + TILE] = incoming[slab, slot * ROWS : (slot + 1) * ROWS, :]


def dot(a, b, ca, cb):
    return lax.dot_general(a, b, (((ca,), (cb,)), ((), ())), preferred_element_type=F32)


def split(value):
    high = value.astype(BF)
    return high, (value - high.astype(F32)).astype(BF)


def gather_parts(parts, count):
    whole = sum(parts[k, : 2 * PART, :].astype(F32) for k in range(count))
    bias = sum(parts[k, 2 * PART :, :].astype(F32) for k in range(count))
    return whole[:PART] + whole[PART:], bias[:4] + bias[4:]


def iota(shape, axis):
    return lax.broadcasted_iota(jnp.int32, shape, axis)


def layer_kernel(
    src,
    dst,
    count,
    first,
    table_hbm,
    adj_hbm,
    w_self_hbm,
    w_neigh_hbm,
    bias_hbm,
    grad_out_hbm,
    act,
    out_hbm,
    grads,
    out,
    table,
    adj,
    w_self,
    w_neigh,
    bias,
    grad_out,
    gathered,
    terms,
    means,
    sems,
):
    def fetch(k, source, target):
        return pltpu.make_async_copy(source, target, sems.at[k])

    get_table = fetch(0, table_hbm, table)
    get_adj = [
        fetch(1 + k, adj_hbm.at[pl.ds(k * FETCH, FETCH)], adj.at[pl.ds(k * FETCH, FETCH)])
        for k in range(FETCHES)
    ]
    rest = [
        fetch(1 + FETCHES + k, source, target)
        for k, (source, target) in enumerate(
            (
                (w_self_hbm, w_self),
                (w_neigh_hbm, w_neigh),
                (bias_hbm, bias),
                (grad_out_hbm, grad_out),
            )
        )
    ]

    get_table.start()
    get_adj[0].start()
    row, col = iota((F, F), 0), iota((F, F), 1)

    x_of, y_of = (col // ROWS) % X, col // (ROWS * X)
    order = (row == x_of * (Y * ROWS) + y_of * ROWS + col % ROWS).astype(F32).astype(BF)
    live = count[0]
    gathered[...] = jnp.zeros_like(gathered)
    terms[...] = jnp.zeros_like(terms)
    ones = jnp.ones((8, GROUP * TILE), BF)
    get_table.wait()
    for copy in get_adj[1:] + rest:
        copy.start()

    def forward(g, carry):
        left, right = [], []
        for j in range(GROUP):
            b = g * GROUP + j
            left.append(table[:, lanes(src[b])])
            block = adj[b]
            alive = b < live
            halves = []
            for t in range(2):
                keep = jnp.where(jnp.logical_and(alive, dst[b] == t), 1.0, 0.0)
                halves.append(block * jnp.full((TILE, TILE), keep, F32).astype(BF))
            right.append(jnp.concatenate(halves, axis=0))
        lhs = jnp.concatenate([jnp.concatenate(left, axis=1), ones], axis=0)
        gathered[...] += dot(lhs, jnp.concatenate(right, axis=1), 1, 1)
        return carry

    groups = lax.div(live + (GROUP - 1), GROUP)
    per = FETCH // GROUP
    for k in range(FETCHES):
        get_adj[k].wait()
        lax.fori_loop(k * per, jnp.minimum(groups, (k + 1) * per), forward, 0)
    for copy in rest:
        copy.wait()
    degree = gathered[F : F + 1, :]
    mean = (gathered[:F, :] / degree).astype(BF)
    start = pl.multiple_of(first[0], OWNED)
    own = table[:, pl.ds(start, OWNED)]
    pre = dot(own, w_self[...], 0, 0) + dot(mean, w_neigh[...], 0, 0) + bias[...]
    sig = jax.nn.sigmoid(pre)
    act[...] = (pre * sig).astype(BF)
    grad_pre = (grad_out[...].astype(F32) * sig * (1.0 + pre * (1.0 - sig))).astype(BF)

    member = 0
    for value in (own, mean):
        both = split(dot(value, grad_pre, 1, 0))
        for k in range(H // TILE):
            for at in range(0, F, PART):
                for half, piece in enumerate(both):
                    grads[member, half * PART : (half + 1) * PART, :] = piece[
                        at : at + PART, k * TILE : (k + 1) * TILE
                    ]
                member += 1
    part_bias = jnp.sum(grad_pre.astype(F32), axis=0, keepdims=True)
    mine = iota((MEMBERS, H), 1) // PER == iota((MEMBERS, H), 0)
    squeeze = (iota((H, TILE), 0) % PER == iota((H, TILE), 1)).astype(F32).astype(BF)
    high, low = (
        dot(jnp.where(mine, value.astype(F32), 0.0).astype(BF), squeeze, 1, 0)
        for value in split(part_bias)
    )
    upper = iota((8, TILE), 0) < 4
    for m in range(MEMBERS):
        grads[m, 2 * PART :, :] = jnp.where(upper, high[m : m + 1], low[m : m + 1]).astype(BF)

    def reorder(value):
        return dot(order, value, 1, 0).astype(BF)

    from_self = dot(reorder(w_self[...]), grad_pre, 1, 1)
    grad_mean = (dot(reorder(w_neigh[...]), grad_pre, 1, 1) / degree).astype(BF)
    means[0] = grad_mean[:, :TILE]
    means[1] = grad_mean[:, TILE:]
    means[2] = jnp.zeros((F, TILE), BF)
    terms[:, pl.ds(start, OWNED)] = from_self

    def backward(g, carry):
        for j in range(GROUP):
            b = g * GROUP + j
            value = means[jnp.where(b < live, dst[b], 2)]
            terms[:, lanes(src[b])] += dot(value, adj[b], 1, 0)
        return carry

    lax.fori_loop(0, groups, backward, 0)

    puts = []
    for n in range(0, COLS, PIECE):
        at = slice(n, n + PIECE)
        out[:, at] = terms[:, at].astype(BF)
        put = pltpu.make_async_copy(out.at[:, at], out_hbm.at[:, at], sems.at[n // PIECE])
        put.start()
        puts.append(put)
    for put in puts:
        put.wait()


def feat_sum_kernel(parts, out):
    whole, bias = gather_parts(parts, MEMBERS)
    high, low = split(whole)
    pair = [value.astype(F32) for value in split(bias)]
    ends = jnp.concatenate(pair, axis=0).astype(BF)
    for k in range(SLABS):
        out[k, :PART, :] = high
        out[k, PART : 2 * PART, :] = low
        out[k, 2 * PART :, :] = ends


def vert_sum_kernel(parts, out):
    whole, bias = gather_parts(parts, SLABS)
    out[:PART, :] = whole
    out[PART : PART + 8, :] = jnp.concatenate([bias, bias], axis=0)
    out[PART + 8 :, :] = jnp.zeros((TOTAL - PART - 8, TILE), F32)


def cut_kernel(terms, out):
    for y in range(Y):
        out[y] = terms[y * ROWS : (y + 1) * ROWS, :]


def sum_kernel(parts, own, away):
    def total(at, width):
        return sum(parts[y, :, at : at + width].astype(F32) for y in range(Y))

    for at in range(0, OWN_COLS, 1024):
        own[:, at : at + 1024] = total(at, 1024)
    for slab in range(SLABS):
        for slot in range(SLOTS):
            tile = total(OWN_COLS + (slab * SLOTS + slot) * TILE, TILE)
            away[slab, slot * ROWS : (slot + 1) * ROWS, :] = tile.astype(BF)


def land_kernel(send, own, back, out):
    out[...] = own[...]
    for slab in range(SLABS):
        for slot in range(SLOTS):
            tile = back[slab, slot * ROWS : (slot + 1) * ROWS, :].astype(F32)
            out[:, lanes(send[slot, slab])] += tile


def unpack_kernel(parts, grad_self, grad_neigh, grad_bias):
    bias = [jnp.zeros((1, TILE), F32) for _ in range(H // TILE)]
    for m in range(MEMBERS):
        block, at = divmod(m * PART, F)
        target = (grad_self, grad_neigh)[block // 2]
        lane = (block % 2) * TILE
        target[at : at + PART, lane : lane + TILE] = parts[m, :PART, :]
        half, lane = divmod(m * PER, TILE)
        bias[half] += pltpu.roll(parts[m, PART : PART + 8, :], lane, 1)[:1]
    for half in range(H // TILE):
        grad_bias[:, half * TILE : (half + 1) * TILE] = bias[half]


def local(
    node_feats,
    w_self,
    w_neigh,
    out_bias,
    adjacency,
    block_dst,
    block_src,
    block_count,
    send_list,
    grad_out,
):
    vert, feat = ("z", "c"), ("y", "x")
    send = jnp.swapaxes(send_list[0], 0, 1)
    first = (lax.axis_index(feat) * OWNED).astype(jnp.int32).reshape(1)
    outgoing, feats = call(
        pick_kernel,
        [SMEM, VMEM],
        (struct((SLABS, SLOTS * ROWS, TILE), BF), struct((ROWS, OWN_COLS), BF)),
    )(send, node_feats)
    incoming = lax.all_to_all(outgoing, vert, 0, 0, tiled=True)
    table = call(table_kernel, [VMEM, VMEM], struct((ROWS, COLS), BF))(feats, incoming)
    table = lax.all_gather(table, "x", axis=0, tiled=True)
    table = lax.all_gather(table, "y", axis=0, tiled=True)
    activated, terms, grads = call(
        layer_kernel,
        [SMEM] * 4 + [HBM] * 6,
        (struct((OWNED, H), BF), struct((F, COLS), BF), struct((MEMBERS, CHUNK, TILE), BF)),
        (
            pltpu.VMEM((F, COLS), BF),
            pltpu.VMEM((F, COLS), BF),
            pltpu.VMEM((BPD, TILE, TILE), BF),
            pltpu.VMEM((F, H), BF),
            pltpu.VMEM((F, H), BF),
            pltpu.VMEM((1, H), F32),
            pltpu.VMEM((OWNED, H), BF),
            pltpu.VMEM((F + 8, OWNED), F32),
            pltpu.VMEM((F, COLS), F32),
            pltpu.VMEM((3, F, TILE), BF),
            pltpu.SemaphoreType.DMA((1 + FETCHES + 4,)),
        ),
        (VMEM, HBM, VMEM),
        FULL_LIMIT,
    )(
        block_src,
        block_dst,
        block_count,
        first,
        table,
        adjacency,
        w_self,
        w_neigh,
        out_bias.reshape(1, H),
        grad_out,
    )
    terms = lax.psum_scatter(terms, "x", scatter_dimension=0, tiled=True)
    grads = lax.all_to_all(grads, feat, 0, 0, tiled=True)
    grads = call(feat_sum_kernel, [VMEM], struct((SLABS, CHUNK, TILE), BF))(grads)
    grads = lax.all_to_all(grads, vert, 0, 0, tiled=True)
    grads = call(vert_sum_kernel, [VMEM], struct((TOTAL, TILE), F32))(grads)
    terms, grads = lax.optimization_barrier((terms, grads))
    grads = lax.all_gather(grads, feat, axis=0, tiled=False)
    terms = call(cut_kernel, [VMEM], struct((Y, ROWS, COLS), BF))(terms)
    terms = lax.all_to_all(terms, "y", 0, 0, tiled=True)
    own, away = call(
        sum_kernel,
        [VMEM],
        (struct((ROWS, OWN_COLS), F32), struct((SLABS, SLOTS * ROWS, TILE), BF)),
    )(terms)
    back = lax.all_to_all(away, vert, 0, 0, tiled=True)
    grad_feats = call(land_kernel, [SMEM, VMEM, VMEM], struct((ROWS, OWN_COLS), F32))(
        send, own, back
    )
    grad_self, grad_neigh, grad_bias = call(
        unpack_kernel,
        [VMEM],
        (struct((F, H), F32), struct((F, H), F32), struct((1, H), F32)),
    )(grads)
    return activated, grad_feats, grad_self, grad_neigh, grad_bias.reshape(H)


def solution(mesh):
    grid = Mesh(mesh.devices.reshape(Z, C, Y, X), ("z", "c", "y", "x"))
    vert, feat = ("z", "c"), ("y", "x")
    every = vert + feat
    in_specs = (
        P(feat, vert),
        P(),
        P(),
        P(),
        P(every, None, None),
        P(every),
        P(every),
        P(every),
        P(vert, None, None),
        P(every, None),
    )
    out_specs = (P(every, None), P(feat, vert), P(), P(), P())
    return jax.shard_map(local, mesh=grid, in_specs=in_specs, out_specs=out_specs, check_vma=False)
```

```python
import functools

import jax
import jax.numpy as jnp
from jax import lax
from jax.experimental import pallas as pl
from jax.experimental.pallas import tpu as pltpu
from jax.sharding import Mesh
from jax.sharding import PartitionSpec as P

X, Y, Z, C = 4, 8, 12, 2
MEMBERS = X * Y
SLABS = Z * C
F = 128
H = 256
TILE = 128
SLOTS = 2
OWN = 64
AWAY = SLABS * SLOTS
TABLE = OWN + AWAY
ROWS = F // MEMBERS
BPD = 96
OWNED = 2 * TILE
COLS = TABLE * TILE
OWN_COLS = OWN * TILE
AWAY_COLS = AWAY * TILE
PART = 16
CHUNK = 2 * PART + 8
TOTAL = PART + 8
PER = H // MEMBERS
EXTRA = X * PART // ROWS * TILE + TILE
GROUP = 24
FETCHES = 4
FETCH = BPD // FETCHES
PIECE = COLS // 7

BF = jnp.bfloat16
F32 = jnp.float32
VMEM = pl.BlockSpec(memory_space=pltpu.VMEM)
SMEM = pl.BlockSpec(memory_space=pltpu.SMEM)
HBM = pl.BlockSpec(memory_space=pltpu.HBM)
LIMIT = 40 * 1024 * 1024
FULL_LIMIT = 62 * 1024 * 1024


def call(body, ins, outs, scratch=(), places=None, limit=LIMIT):
    return pl.pallas_call(
        body,
        in_specs=ins,
        out_specs=jax.tree.map(lambda _: VMEM, outs) if places is None else places,
        out_shape=outs,
        scratch_shapes=scratch,
        compiler_params=pltpu.CompilerParams(vmem_limit_bytes=limit),
    )


def struct(shape, dtype):
    return jax.ShapeDtypeStruct(shape, dtype)


def lanes(at):
    return pl.ds(pl.multiple_of(at * TILE, TILE), TILE)


def pick_kernel(send, feats, out, same):
    same[...] = feats[...]
    for slab in range(SLABS):
        for slot in range(SLOTS):
            tile = feats[:, lanes(send[slot, slab])]
            out[slab, slot * ROWS : (slot + 1) * ROWS, :] = tile


def table_kernel(feats, incoming, out):
    out[:, :OWN_COLS] = feats[...]
    for slab in range(SLABS):
        for slot in range(SLOTS):
            at = OWN_COLS + (slab * SLOTS + slot) * TILE
            out[:, at : at + TILE] = incoming[slab, slot * ROWS : (slot + 1) * ROWS, :]


def dot(a, b, ca, cb):
    return lax.dot_general(a, b, (((ca,), (cb,)), ((), ())), preferred_element_type=F32)


def split(value):
    high = value.astype(BF)
    return high, (value - high.astype(F32)).astype(BF)


def gather_parts(parts, count):
    whole = sum(parts[k, : 2 * PART, :].astype(F32) for k in range(count))
    bias = sum(parts[k, 2 * PART :, :].astype(F32) for k in range(count))
    return whole[:PART] + whole[PART:], bias[:4] + bias[4:]


def iota(shape, axis):
    return lax.broadcasted_iota(jnp.int32, shape, axis)


def layer_kernel(
    src,
    dst,
    count,
    first,
    table_hbm,
    adj_hbm,
    w_self_hbm,
    w_neigh_hbm,
    bias_hbm,
    grad_out_hbm,
    act,
    out_hbm,
    grads,
    out,
    table,
    adj,
    w_self,
    w_neigh,
    bias,
    grad_out,
    gathered,
    terms,
    means,
    sems,
):
    def fetch(k, source, target):
        return pltpu.make_async_copy(source, target, sems.at[k])

    get_table = fetch(0, table_hbm, table)
    get_adj = [
        fetch(1 + k, adj_hbm.at[pl.ds(k * FETCH, FETCH)], adj.at[pl.ds(k * FETCH, FETCH)])
        for k in range(FETCHES)
    ]
    rest = [
        fetch(1 + FETCHES + k, source, target)
        for k, (source, target) in enumerate(
            (
                (w_self_hbm, w_self),
                (w_neigh_hbm, w_neigh),
                (bias_hbm, bias),
                (grad_out_hbm, grad_out),
            )
        )
    ]

    get_table.start()
    get_adj[0].start()
    row, col = iota((F, F), 0), iota((F, F), 1)

    x_of, y_of = (col // ROWS) % X, col // (ROWS * X)
    order = (row == x_of * (Y * ROWS) + y_of * ROWS + col % ROWS).astype(F32).astype(BF)
    live = count[0]
    gathered[...] = jnp.zeros_like(gathered)
    terms[...] = jnp.zeros_like(terms)
    ones = jnp.ones((8, GROUP * TILE), BF)
    get_table.wait()
    for copy in get_adj[1:] + rest:
        copy.start()

    def forward(g, carry):
        left, right = [], []
        for j in range(GROUP):
            b = g * GROUP + j
            left.append(table[:, lanes(src[b])])
            block = adj[b]
            alive = b < live
            halves = []
            for t in range(2):
                keep = jnp.where(jnp.logical_and(alive, dst[b] == t), 1.0, 0.0)
                halves.append(block * jnp.full((TILE, TILE), keep, F32).astype(BF))
            right.append(jnp.concatenate(halves, axis=0))
        lhs = jnp.concatenate([jnp.concatenate(left, axis=1), ones], axis=0)
        gathered[...] += dot(lhs, jnp.concatenate(right, axis=1), 1, 1)
        return carry

    groups = lax.div(live + (GROUP - 1), GROUP)
    per = FETCH // GROUP
    for k in range(FETCHES):
        get_adj[k].wait()
        lax.fori_loop(k * per, jnp.minimum(groups, (k + 1) * per), forward, 0)
    for copy in rest:
        copy.wait()
    degree = gathered[F : F + 1, :]
    mean = (gathered[:F, :] / degree).astype(BF)
    start = pl.multiple_of(first[0], OWNED)
    own = table[:, pl.ds(start, OWNED)]
    pre = dot(own, w_self[...], 0, 0) + dot(mean, w_neigh[...], 0, 0) + bias[...]
    sig = jax.nn.sigmoid(pre)
    act[...] = (pre * sig).astype(BF)
    grad_pre = (grad_out[...].astype(F32) * sig * (1.0 + pre * (1.0 - sig))).astype(BF)

    member = 0
    for value in (own, mean):
        both = split(dot(value, grad_pre, 1, 0))
        for k in range(H // TILE):
            for at in range(0, F, PART):
                for half, piece in enumerate(both):
                    grads[member, half * PART : (half + 1) * PART, :] = piece[
                        at : at + PART, k * TILE : (k + 1) * TILE
                    ]
                member += 1
    part_bias = jnp.sum(grad_pre.astype(F32), axis=0, keepdims=True)
    mine = iota((MEMBERS, H), 1) // PER == iota((MEMBERS, H), 0)
    squeeze = (iota((H, TILE), 0) % PER == iota((H, TILE), 1)).astype(F32).astype(BF)
    high, low = (
        dot(jnp.where(mine, value.astype(F32), 0.0).astype(BF), squeeze, 1, 0)
        for value in split(part_bias)
    )
    upper = iota((8, TILE), 0) < 4
    for m in range(MEMBERS):
        grads[m, 2 * PART :, :] = jnp.where(upper, high[m : m + 1], low[m : m + 1]).astype(BF)

    def reorder(value):
        return dot(order, value, 1, 0).astype(BF)

    from_self = dot(reorder(w_self[...]), grad_pre, 1, 1)
    grad_mean = (dot(reorder(w_neigh[...]), grad_pre, 1, 1) / degree).astype(BF)
    means[0] = grad_mean[:, :TILE]
    means[1] = grad_mean[:, TILE:]
    means[2] = jnp.zeros((F, TILE), BF)
    terms[:, pl.ds(start, OWNED)] = from_self

    def backward(g, carry):
        for j in range(GROUP):
            b = g * GROUP + j
            value = means[jnp.where(b < live, dst[b], 2)]
            terms[:, lanes(src[b])] += dot(value, adj[b], 1, 0)
        return carry

    lax.fori_loop(0, groups, backward, 0)

    puts = []
    for n in range(0, COLS, PIECE):
        at = slice(n, n + PIECE)
        out[:, at] = terms[:, at].astype(BF)
        put = pltpu.make_async_copy(out.at[:, at], out_hbm.at[:, at], sems.at[n // PIECE])
        put.start()
        puts.append(put)
    for put in puts:
        put.wait()


def feat_sum_kernel(parts, out):
    whole, bias = gather_parts(parts, MEMBERS)
    high, low = split(whole)
    pair = [value.astype(F32) for value in split(bias)]
    ends = jnp.concatenate(pair, axis=0).astype(BF)
    for k in range(SLABS):
        out[k, :PART, :] = high
        out[k, PART : 2 * PART, :] = low
        out[k, 2 * PART :, :] = ends


def vert_sum_kernel(parts, out):
    whole, bias = gather_parts(parts, SLABS)
    out[:PART, :] = whole
    out[PART:, :] = jnp.concatenate([bias, bias], axis=0)


def join_kernel(terms, grads, out):
    for y in range(Y):
        out[y, :, :COLS] = terms[y * ROWS : (y + 1) * ROWS, :]
    at = COLS
    for x in range(X):
        for k in range(0, PART, ROWS):
            value = grads[x, k : k + ROWS, :].astype(BF)
            for y in range(Y):
                out[y, :, at : at + TILE] = value
            at += TILE
    bias = grads[0, PART : PART + ROWS, :]
    for x in range(1, X):
        bias += pltpu.roll(grads[x, PART : PART + ROWS, :], x * PER, 1)
    for y in range(Y):
        out[y, :, at:] = bias.astype(BF)


def sum_kernel(parts, own, away, extra):
    def total(at, width):
        return sum(parts[y, :, at : at + width].astype(F32) for y in range(Y))

    for at in range(0, OWN_COLS, 1024):
        own[:, at : at + 1024] = total(at, 1024)
    for slab in range(SLABS):
        for slot in range(SLOTS):
            tile = total(OWN_COLS + (slab * SLOTS + slot) * TILE, TILE)
            away[slab, slot * ROWS : (slot + 1) * ROWS, :] = tile.astype(BF)
    for y in range(Y):
        extra[y] = parts[y, :, COLS:]


def land_kernel(send, own, back, extra, out, grad_self, grad_neigh, grad_bias):
    out[...] = own[...]
    for slab in range(SLABS):
        for slot in range(SLOTS):
            tile = back[slab, slot * ROWS : (slot + 1) * ROWS, :].astype(F32)
            out[:, lanes(send[slot, slab])] += tile
    pieces = X * PART // ROWS
    for y in range(Y):
        block, at = divmod(y * X * PART, F)
        target = (grad_self, grad_neigh)[block // 2]
        lane = (block % 2) * TILE
        for k in range(0, pieces, 2):
            value = jnp.concatenate(
                [extra[y, :, j * TILE : (j + 1) * TILE].astype(F32) for j in (k, k + 1)], axis=0
            )
            target[at + k * ROWS : at + (k + 2) * ROWS, lane : lane + TILE] = value
    each = X * PER
    for half in range(H // TILE):
        first = half * (TILE // each)
        value = extra[first, :, pieces * TILE :].astype(F32)
        for k in range(1, TILE // each):
            value += pltpu.roll(extra[first + k, :, pieces * TILE :].astype(F32), k * each, 1)
        grad_bias[:, half * TILE : (half + 1) * TILE] = value[:1]


def local(
    node_feats,
    w_self,
    w_neigh,
    out_bias,
    adjacency,
    block_dst,
    block_src,
    block_count,
    send_list,
    grad_out,
):
    vert, feat = ("z", "c"), ("y", "x")
    send = jnp.swapaxes(send_list[0], 0, 1)
    first = (lax.axis_index(feat) * OWNED).astype(jnp.int32).reshape(1)
    outgoing, feats = call(
        pick_kernel,
        [SMEM, VMEM],
        (struct((SLABS, SLOTS * ROWS, TILE), BF), struct((ROWS, OWN_COLS), BF)),
    )(send, node_feats)
    incoming = lax.all_to_all(outgoing, vert, 0, 0, tiled=True)
    table = call(table_kernel, [VMEM, VMEM], struct((ROWS, COLS), BF))(feats, incoming)
    table = lax.all_gather(table, "x", axis=0, tiled=True)
    table = lax.all_gather(table, "y", axis=0, tiled=True)
    activated, terms, grads = call(
        layer_kernel,
        [SMEM] * 4 + [HBM] * 6,
        (struct((OWNED, H), BF), struct((F, COLS), BF), struct((MEMBERS, CHUNK, TILE), BF)),
        (
            pltpu.VMEM((F, COLS), BF),
            pltpu.VMEM((F, COLS), BF),
            pltpu.VMEM((BPD, TILE, TILE), BF),
            pltpu.VMEM((F, H), BF),
            pltpu.VMEM((F, H), BF),
            pltpu.VMEM((1, H), F32),
            pltpu.VMEM((OWNED, H), BF),
            pltpu.VMEM((F + 8, OWNED), F32),
            pltpu.VMEM((F, COLS), F32),
            pltpu.VMEM((3, F, TILE), BF),
            pltpu.SemaphoreType.DMA((1 + FETCHES + 4,)),
        ),
        (VMEM, HBM, VMEM),
        FULL_LIMIT,
    )(
        block_src,
        block_dst,
        block_count,
        first,
        table,
        adjacency,
        w_self,
        w_neigh,
        out_bias.reshape(1, H),
        grad_out,
    )
    terms = lax.psum_scatter(terms, "x", scatter_dimension=0, tiled=True)
    grads = lax.all_to_all(grads, feat, 0, 0, tiled=True)
    grads = call(feat_sum_kernel, [VMEM], struct((SLABS, CHUNK, TILE), BF))(grads)
    grads = lax.all_to_all(grads, vert, 0, 0, tiled=True)
    grads = call(vert_sum_kernel, [VMEM], struct((TOTAL, TILE), F32))(grads)
    grads = lax.all_gather(grads, "x", axis=0, tiled=False)
    terms, grads = lax.optimization_barrier((terms, grads))
    terms = call(join_kernel, [VMEM, VMEM], struct((Y, ROWS, COLS + EXTRA), BF))(terms, grads)
    terms = lax.all_to_all(terms, "y", 0, 0, tiled=True)
    own, away, extra = call(
        sum_kernel,
        [VMEM],
        (
            struct((ROWS, OWN_COLS), F32),
            struct((SLABS, SLOTS * ROWS, TILE), BF),
            struct((Y, ROWS, EXTRA), BF),
        ),
    )(terms)
    back = lax.all_to_all(away, vert, 0, 0, tiled=True)
    grad_feats, grad_self, grad_neigh, grad_bias = call(
        land_kernel,
        [SMEM, VMEM, VMEM, VMEM],
        (
            struct((ROWS, OWN_COLS), F32),
            struct((F, H), F32),
            struct((F, H), F32),
            struct((1, H), F32),
        ),
    )(send, own, back, extra)
    return activated, grad_feats, grad_self, grad_neigh, grad_bias.reshape(H)


def solution(mesh):
    grid = Mesh(mesh.devices.reshape(Z, C, Y, X), ("z", "c", "y", "x"))
    vert, feat = ("z", "c"), ("y", "x")
    every = vert + feat
    in_specs = (
        P(feat, vert),
        P(),
        P(),
        P(),
        P(every, None, None),
        P(every),
        P(every),
        P(every),
        P(vert, None, None),
        P(every, None),
    )
    out_specs = (P(every, None), P(feat, vert), P(), P(), P())
    return jax.shard_map(local, mesh=grid, in_specs=in_specs, out_specs=out_specs, check_vma=False)
```
